128 devices in a mesh: slab: 16 (over x, y), sec: 8 (over z, core).
Axes of the slice: x: 4, y: 4, z: 4, core: 2. Of those that a mesh axis runs over, the one named last changes fastest.
Arguments:
- coefficients: float32 [17, 12, 147456], P(None, None, ('slab', 'sec')), may hold values from -2.4 to 2.4
- azimuths: float32 [8, 147456], P(None, ('slab', 'sec')), may hold values from -3.140625 to 3.140625
- route_rows: int32 [128, 128, 12], P(('slab', 'sec')), may hold values from 0 to 1152, as said below
- face_points: int32 [128, 128, 64], P(('slab', 'sec')), may hold values from 0 to 12288, as said below
- face_nodes: int32 [128, 128, 64], P(('slab', 'sec')), may hold values from 0 to 9600, as said below
- disp_start: float32 [3, 1228800], P(None, ('slab', 'sec')), may hold values from -6 to 6
- veloc_start: float32 [3, 1228800], P(None, ('slab', 'sec')), may hold values from -6 to 6
- memory_start: float32 [9, 125, 16384], P(None, None, ('slab', 'sec')), may hold values from -6 to 6
- connectivity: int32 [125, 16384], P(None, ('slab', 'sec')), may hold values from 0 to 9599, as said below
- x_shared: int32 [2, 71808], P(None, ('slab', 'sec')), may hold values from 0 to 9599, as said below
- y_shared: int32 [2, 71808], P(None, ('slab', 'sec')), may hold values from 0 to 9599, as said below
- absorbing: int32 [16384], P(('slab', 'sec')), may hold values from 0 to 1, as said below
- damping: float32 [16384], P(('slab', 'sec')), may hold values from 0.5 to 10
- modulus: float32 [16384], P(('slab', 'sec')), may hold values from 0.1 to 0.4
- masses: float32 [1228800], P(('slab', 'sec')), may hold values from 1 to 4
Outputs:
- displacement: float32 [3, 1228800], P(None, ('slab', 'sec'))
- velocity: float32 [3, 1228800], P(None, ('slab', 'sec'))
The draws below stay inside these ranges and needn't reach their ends.
Inputs may be any that keep to these rules, and one draw needn't show every extreme that they name: `route_rows`: 1152 means an empty slot; each source's list holds each of its rows 0..1151 exactly once; some owner receives 12 rows from every source. `face_points`: 12288 means no point. `face_nodes`: 9600 means no node. `connectivity`: local node numbers of a conforming hexahedral GLL mesh, neighbouring elements sharing their face nodes. `x_shared`: local node numbers; entry k of a partition's row 1 is the same physical node as entry k of the next partition's row 0. `y_shared`: local node numbers; entry k of a partition's row 1 is the same physical node as entry k of the next partition's row 0. `absorbing`: 1 marks a bottom layer of one to three elements under each element column of each partition, and outer side layers of one or two elements whose thickness each partition draws for itself.
All inputs are finite; a program needn't handle non-finite values.
Results may differ from the reference program's by a relative error of at most 0.0001.
Values sent between devices are 32-bit elements; how exact they have to be, the bound alone decides.
A program may use at most 128 MiB of HBM per device.

```python
import math
import jax
import jax.numpy as jnp
import numpy as np
from jax import lax

EX = 4
EY = 4
EZ = 8
NCOEF = 17
STEPS = 4
AZ = 8
CAP = 12
CAP2 = 64
GR = 1152
NE = 128
NN = 9600
SHX = 561
SHY = 561
POINTS = 12288
GTOT = 147456
NE_TOT = 16384
NN_TOT = 1228800
N_SLAB = 16
N_SEC = 8


def mesh_tables(key):
    devices = N_SLAB * N_SEC
    keys = jax.random.split(key, 3)
    node_perm = jax.vmap(lambda sub: jax.random.permutation(sub, NN))(jax.random.split(keys[0], devices))
    x_order = jax.vmap(lambda sub: jax.random.permutation(sub, SHX))(jax.random.split(keys[1], devices))
    y_order = jax.vmap(lambda sub: jax.random.permutation(sub, SHY))(jax.random.split(keys[2], devices))
    return (node_perm.astype(jnp.int32), x_order.astype(jnp.int32), y_order.astype(jnp.int32))


def structured(first, second, third):
    return ((first * (4 * EY + 1) + second) * (4 * EZ + 1) + third).astype(jnp.int32)


def element_grid():
    element = jnp.arange(NE, dtype=jnp.int32)
    return (element // (EY * EZ), element // EZ % EY, element % EZ)


def draw_connectivity(key, part):
    node_perm, x_order, y_order = mesh_tables(key)
    local_pt = jnp.arange(125, dtype=jnp.int32)
    along_i = local_pt // 25
    along_j = local_pt // 5 % 5
    along_k = local_pt % 5
    elem_x, elem_y, elem_z = element_grid()
    struct_ids = structured(4 * elem_x[None, :] + along_i[:, None], 4 * elem_y[None, :] + along_j[:, None], 4 * elem_z[None, :] + along_k[:, None])
    mapped = jnp.take(node_perm, struct_ids.reshape(-1), axis=1).reshape(N_SLAB * N_SEC, 125, NE)
    return mapped.transpose(1, 0, 2).reshape(125, -1)


def draw_x_shared(key, part):
    node_perm, x_order, y_order = mesh_tables(key)
    devices = N_SLAB * N_SEC
    face = jnp.arange(SHX, dtype=jnp.int32)
    lower_ids = structured(face * 0, face // (4 * EZ + 1), face % (4 * EZ + 1))
    upper_ids = structured(face * 0 + 4 * EX, face // (4 * EZ + 1), face % (4 * EZ + 1))
    device = jnp.arange(devices, dtype=jnp.int32)
    before = jnp.where(device >= N_SEC, device - N_SEC, device)
    lower = jnp.take_along_axis(node_perm, lower_ids[x_order[before]], axis=1)
    upper = jnp.take_along_axis(node_perm, upper_ids[x_order], axis=1)
    return jnp.stack([lower, upper], axis=1).transpose(1, 0, 2).reshape(2, -1)


def draw_y_shared(key, part):
    node_perm, x_order, y_order = mesh_tables(key)
    devices = N_SLAB * N_SEC
    face = jnp.arange(SHY, dtype=jnp.int32)
    lower_ids = structured(face // (4 * EZ + 1), face * 0, face % (4 * EZ + 1))
    upper_ids = structured(face // (4 * EZ + 1), face * 0 + 4 * EY, face % (4 * EZ + 1))
    device = jnp.arange(devices, dtype=jnp.int32)
    before = jnp.where(device % N_SEC > 0, device - 1, device)
    lower = jnp.take_along_axis(node_perm, lower_ids[y_order[before]], axis=1)
    upper = jnp.take_along_axis(node_perm, upper_ids[y_order], axis=1)
    return jnp.stack([lower, upper], axis=1).transpose(1, 0, 2).reshape(2, -1)


def draw_absorbing(key, part):
    key = jax.random.fold_in(key, 21)
    keys = jax.random.split(key, 2)
    devices = N_SLAB * N_SEC
    bottom = jax.random.randint(keys[0], (devices, EX * EY), 1, 4)
    side = jax.random.randint(keys[1], (devices, 1), 1, 3)
    device = jnp.arange(devices, dtype=jnp.int32)[:, None]
    slab_pos = device // N_SEC
    sec_pos = device % N_SEC
    elem_x, elem_y, elem_z = element_grid()
    column = elem_x * EY + elem_y
    depth_limit = jnp.take(bottom, column, axis=1)
    elem_x = elem_x[None, :]
    elem_y = elem_y[None, :]
    elem_z = elem_z[None, :]
    flagged = (elem_z < depth_limit) | (slab_pos == 0) & (elem_x < side) | (slab_pos == N_SLAB - 1) & (elem_x >= EX - side)
    flagged = flagged | (sec_pos == 0) & (elem_y < side) | (sec_pos == N_SEC - 1) & (elem_y >= EY - side)
    return flagged.astype(jnp.int32).reshape(-1)


def draw_route_rows(key, part):
    key = jax.random.fold_in(key, 31)
    devices = N_SLAB * N_SEC
    slots = devices * CAP
    keys = jax.random.split(key, 3)
    bias = jax.random.randint(keys[0], (devices,), 0, 2 ** 11)
    favoured = jax.random.randint(keys[1], (), 0, devices)
    owner = jnp.arange(devices, dtype=jnp.int32)

    def per_source(sub):
        first, second = jax.random.split(sub)
        score = jax.random.randint(first, (devices, CAP), 0, 2 ** 12) + bias[:, None] + jnp.where(owner[:, None] == favoured, 2 ** 13, 0)
        flat = score.reshape(-1) * slots + jnp.arange(slots, dtype=jnp.int32)
        order = jnp.argsort(-flat, stable=True)
        rows = jax.random.permutation(second, GR).astype(jnp.int32)
        filled = jnp.full((slots,), GR, jnp.int32).at[order[:GR]].set(rows)
        return filled.reshape(devices, CAP)
    return jax.vmap(per_source)(jax.random.split(keys[2], devices))


def draw_face_points(key, part):
    key = jax.random.fold_in(key, 41)
    devices = N_SLAB * N_SEC
    keys = jax.random.split(key, 2)
    values = jax.random.randint(keys[0], (devices, devices, CAP2), 0, POINTS)
    empty = jax.random.randint(keys[1], (devices, devices, CAP2), 0, 4) == 0
    values = jnp.where(empty, POINTS, values)
    return values.at[:, :, CAP2 - 1].set(POINTS).astype(jnp.int32)


def draw_face_nodes(key, part):
    key = jax.random.fold_in(key, 51)
    devices = N_SLAB * N_SEC
    keys = jax.random.split(key, 2)
    values = jax.random.randint(keys[0], (devices, devices, CAP2), 0, NN)
    empty = jax.random.randint(keys[1], (devices, devices, CAP2), 0, 4) == 0
    values = jnp.where(empty, NN, values)
    return values.at[:, :, CAP2 - 1].set(NN).astype(jnp.int32)


def level_of(stream_key, shape, shards, low, high):
    loudness, own = 1.0, jax.random.fold_in(stream_key, 6)
    for dim, blocks in shards:
        steps = jnp.exp(jax.random.uniform(jax.random.fold_in(own, dim), (blocks,), jnp.float32, low / len(shards), high / len(shards)))
        loudness = loudness * jnp.repeat(steps, shape[dim] // blocks).reshape([-1 if axis == dim else 1 for axis in range(len(shape))])
    return loudness


def centred(own_key, dims, scale, most, cuts=(), kind=jnp.bfloat16):
    values = scale * jax.random.normal(own_key, dims, jnp.float32)
    if cuts:
        values = values * level_of(own_key, dims, cuts, -0.22, 0.18)
    return jnp.clip(values, -most, most).astype(kind)


def setup_inputs(seed: int = 0) -> dict:
    seeds = jax.random.split(jax.random.key(seed), 16)
    coefficients = centred(seeds[0], (NCOEF, 3 * STEPS, GTOT), 0.3, 2.4, ((2, 128),), jnp.float32)
    azimuths = jnp.clip(jax.random.uniform(seeds[1], (AZ, GTOT), jnp.float32, -3.140625, 3.140625), -3.140625, 3.140625)
    route_rows = draw_route_rows(jax.random.fold_in(seeds[15], 71), 0)
    face_points = draw_face_points(jax.random.fold_in(seeds[15], 71), 0)
    face_nodes = draw_face_nodes(jax.random.fold_in(seeds[15], 71), 0)
    disp_start = centred(seeds[5], (3, NN_TOT), 1.0, 6.0, ((1, 128),), jnp.float32)
    veloc_start = centred(seeds[6], (3, NN_TOT), 1.0, 6.0, ((1, 128),), jnp.float32)
    memory_start = centred(seeds[7], (9, 125, NE_TOT), 1.0, 6.0, ((2, 128),), jnp.float32)
    connectivity = draw_connectivity(jax.random.fold_in(seeds[15], 71), 0)
    x_shared = draw_x_shared(jax.random.fold_in(seeds[15], 71), 0)
    y_shared = draw_y_shared(jax.random.fold_in(seeds[15], 71), 0)
    absorbing = draw_absorbing(jax.random.fold_in(seeds[15], 71), 0)
    damping = jnp.clip(jnp.exp(math.log(10.0) - 2.9957323 * jax.random.uniform(seeds[12], (NE_TOT,), jnp.float32) ** level_of(seeds[12], (NE_TOT,), ((0, 128),), -0.2, 0.2)), 0.5, 10.0)
    modulus = jnp.clip(jnp.exp(math.log(0.4) - 1.3862944 * jax.random.uniform(seeds[13], (NE_TOT,), jnp.float32) ** level_of(seeds[13], (NE_TOT,), ((0, 128),), -0.2, 0.2)), 0.1, 0.4)
    masses = jnp.clip(jnp.exp(math.log(4.0) - 1.3862944 * jax.random.uniform(seeds[14], (NN_TOT,), jnp.float32) ** level_of(seeds[14], (NN_TOT,), ((0, 128),), -0.2, 0.2)), 1.0, 4.0)
    return {"coefficients": coefficients, "azimuths": azimuths, "route_rows": route_rows, "face_points": face_points, "face_nodes": face_nodes, "disp_start": disp_start, "veloc_start": veloc_start, "memory_start": memory_start, "connectivity": connectivity, "x_shared": x_shared, "y_shared": y_shared, "absorbing": absorbing, "damping": damping, "modulus": modulus, "masses": masses}


time_step = 0.1

def gll_tables():
    points = np.array([-1.0, -math.sqrt(3.0 / 7.0), 0.0, math.sqrt(3.0 / 7.0), 1.0])
    weights = np.array([0.1, 49.0 / 90.0, 32.0 / 45.0, 49.0 / 90.0, 0.1])
    products = np.array([np.prod([points[row_idx] - points[col_idx] for col_idx in range(5) if col_idx != row_idx]) for row_idx in range(5)])
    derivative = np.zeros((5, 5))
    for row_idx in range(5):
        for col_idx in range(5):
            if row_idx != col_idx:
                derivative[row_idx, col_idx] = products[row_idx] / (products[col_idx] * (points[row_idx] - points[col_idx]))
        derivative[row_idx, row_idx] = -derivative[row_idx].sum()
    weight_cube = weights[:, None, None] * weights[None, :, None] * weights[None, None, :]
    return (jnp.asarray(derivative, jnp.float32), jnp.asarray(weight_cube, jnp.float32))

def element_force(field, memory, connect, modulus, absorb, retain, derivative, weight_cube):
    node_count = field.shape[1]
    elements = connect.shape[1]
    highest = lax.Precision.HIGHEST
    element_values = jnp.take(field, connect.reshape(-1), axis=1).reshape(3, 5, 5, 5, elements)
    grad_x = jnp.einsum('ia,cajke->cijke', derivative, element_values, precision=highest)
    grad_y = jnp.einsum('jb,cibke->cijke', derivative, element_values, precision=highest)
    grad_z = jnp.einsum('kz,cijze->cijke', derivative, element_values, precision=highest)
    gradients = jnp.stack([grad_x, grad_y, grad_z]).reshape(9, 125, elements)
    weighting = modulus[None, :] * weight_cube.reshape(125, 1)
    stress = weighting[None] * (gradients - absorb[None, None, :] * memory)
    memory_next = absorb * (retain * memory + (1.0 - retain) * gradients)
    stress = stress.reshape(3, 3, 5, 5, 5, elements)
    divergence = jnp.einsum('ai,cajke->cijke', derivative, stress[0], precision=highest)
    divergence = divergence + jnp.einsum('bj,cibke->cijke', derivative, stress[1], precision=highest)
    divergence = divergence + jnp.einsum('zk,cijze->cijke', derivative, stress[2], precision=highest)
    forces = jnp.zeros((3, node_count), jnp.float32).at[:, connect.reshape(-1)].add(-divergence.reshape(3, -1))
    return (forces, memory_next)

def pick_nodes(field_dev, index):
    return field_dev[:, index]

def add_rims(field_dev, lower, upper, before, after):
    return field_dev.at[:, lower].add(before).at[:, upper].add(after)

def shift_forward(values, axis_pos):
    edge = jnp.zeros_like(lax.slice_in_dim(values, 0, 1, axis=axis_pos))
    rest = lax.slice_in_dim(values, 0, values.shape[axis_pos] - 1, axis=axis_pos)
    return jnp.concatenate([edge, rest], axis=axis_pos)

def shift_backward(values, axis_pos):
    edge = jnp.zeros_like(lax.slice_in_dim(values, 0, 1, axis=axis_pos))
    rest = lax.slice_in_dim(values, 1, values.shape[axis_pos], axis=axis_pos)
    return jnp.concatenate([rest, edge], axis=axis_pos)

def assemble_faces(grid, shared, axis_pos):
    lower = shared[:, :, 0]
    upper = shared[:, :, 1]
    picker = jax.vmap(jax.vmap(pick_nodes))
    lower_vals = picker(grid, lower)
    upper_vals = picker(grid, upper)
    from_before = shift_forward(upper_vals, axis_pos)
    from_after = shift_backward(lower_vals, axis_pos)
    return jax.vmap(jax.vmap(add_rims))(grid, lower, upper, from_before, from_after)

def reference(coefficients, azimuths, route_rows, face_points, face_nodes, disp_start, veloc_start, memory_start, connectivity, x_shared, y_shared, absorbing, damping, modulus, masses):
    derivative, weight_cube = gll_tables()
    devices = N_SLAB * N_SEC
    total_rows = GR * devices
    highest = lax.Precision.HIGHEST
    coef_pad = jnp.concatenate([coefficients, jnp.zeros((coefficients.shape[0], coefficients.shape[1], 1), jnp.float32)], axis=2)
    angle_pad = jnp.concatenate([azimuths, jnp.zeros((azimuths.shape[0], 1), jnp.float32)], axis=1)
    owner_major = jnp.transpose(route_rows, (1, 0, 2))
    source = jnp.arange(devices, dtype=jnp.int32)[None, :, None]
    global_index = jnp.where(owner_major < GR, source * GR + owner_major, total_rows).astype(jnp.int32).reshape(devices, devices * CAP)
    owner_rows = jnp.take(coef_pad, global_index, axis=2)
    owner_angles = jnp.take(angle_pad, global_index, axis=1)
    orders = jnp.arange(9, dtype=jnp.float32)
    cosines = jnp.cos(orders[:, None, None, None] * owner_angles[None])
    sines = jnp.sin(orders[1:, None, None, None] * owner_angles[None])
    basis = jnp.concatenate([cosines, sines], axis=0)
    traces = jnp.einsum('ktos,kaos->otas', owner_rows, basis, precision=highest)
    point_rows = traces.reshape(devices, 3 * STEPS, POINTS)
    point_rows = jnp.concatenate([point_rows, jnp.zeros((devices, 3 * STEPS, 1), jnp.float32)], axis=2)
    sent = jax.vmap(lambda rows_one, index: jnp.take(rows_one, index.reshape(-1), axis=1))(point_rows, face_points)
    by_receiver = sent.reshape(devices, 3 * STEPS, devices, CAP2).transpose(2, 1, 0, 3).reshape(devices, 3 * STEPS, devices * CAP2)
    injected = jax.vmap(lambda values, nodes: jnp.zeros((3 * STEPS, NN + 1), jnp.float32).at[:, nodes.reshape(-1)].add(values)[:, :NN])(by_receiver, face_nodes)
    injected = injected.reshape(devices, STEPS, 3, NN)
    field = disp_start.reshape(3, devices, NN).transpose(1, 0, 2)
    veloc = veloc_start.reshape(3, devices, NN).transpose(1, 0, 2)
    memory = memory_start.reshape(9, 125, devices, NE).transpose(2, 0, 1, 3)
    connect = connectivity.reshape(125, devices, NE).transpose(1, 0, 2)
    modulus_dev = modulus.reshape(devices, NE)
    absorb_dev = absorbing.astype(jnp.float32).reshape(devices, NE)
    retain_dev = jnp.exp(-time_step * damping).reshape(devices, NE)
    mass_dev = masses.reshape(devices, NN)
    x_grid = x_shared.reshape(2, devices, SHX).transpose(1, 0, 2).reshape(N_SLAB, N_SEC, 2, SHX)
    y_grid = y_shared.reshape(2, devices, SHY).transpose(1, 0, 2).reshape(N_SLAB, N_SEC, 2, SHY)
    for step in range(STEPS):
        forces, memory = lax.map(lambda parts: element_force(parts[0], parts[1], parts[2], parts[3], parts[4], parts[5], derivative, weight_cube), (field, memory, connect, modulus_dev, absorb_dev, retain_dev))
        forces = forces + injected[:, step]
        grid = forces.reshape(N_SLAB, N_SEC, 3, NN)
        grid = assemble_faces(grid, x_grid, 0)
        grid = assemble_faces(grid, y_grid, 1)
        forces = grid.reshape(devices, 3, NN)
        veloc = veloc + time_step * forces / mass_dev[:, None, :]
        field = field + time_step * veloc
    return (field.transpose(1, 0, 2).reshape(3, -1), veloc.transpose(1, 0, 2).reshape(3, -1))
```

```python
import math

import jax
import jax.numpy as jnp
import numpy as np
from jax import lax
from jax.experimental import pallas as pl
from jax.experimental.pallas import tpu as pltpu
from jax.sharding import PartitionSpec as P

F32 = jnp.float32
BF16 = jnp.bfloat16
HIGHEST = lax.Precision.HIGHEST
MESH = pl.DeviceIdType.MESH
DT = 0.1
VMEM_LIMIT = 56 * 2**20


def gll_tables():
    points = np.array([-1.0, -math.sqrt(3.0 / 7.0), 0.0, math.sqrt(3.0 / 7.0), 1.0])
    weights = np.array([0.1, 49.0 / 90.0, 32.0 / 45.0, 49.0 / 90.0, 0.1])
    products = np.array(
        [np.prod([points[r] - points[c] for c in range(5) if c != r]) for r in range(5)]
    )
    derivative = np.zeros((5, 5))
    for r in range(5):
        for c in range(5):
            if r != c:
                derivative[r, c] = products[r] / (products[c] * (points[r] - points[c]))
        derivative[r, r] = -derivative[r].sum()
    cube = weights[:, None, None] * weights[None, :, None] * weights[None, None, :]
    eye = np.eye(5)
    grad = np.zeros((3, 128, 128))
    grad[0, :125, :125] = np.kron(derivative, np.kron(eye, eye))
    grad[1, :125, :125] = np.kron(eye, np.kron(derivative, eye))
    grad[2, :125, :125] = np.kron(eye, np.kron(eye, derivative))
    grad = grad.reshape(384, 128).astype(np.float32)
    cube128 = np.zeros((128, 128), np.float32)
    cube128[:125] = cube.reshape(125, 1)
    return grad, np.ascontiguousarray(grad.T), cube128


def split2(x):
    hi = x.astype(BF16)
    return hi, (x - hi.astype(F32)).astype(BF16)


def halves(low, high):
    return jnp.concatenate([low, high], axis=1)


def lanes_of_rows(ref, start, count):
    return jnp.concatenate([ref[pl.ds(start + q, 1), :] for q in range(count)], axis=1)


def one_hot(low, width):
    iota = lax.broadcasted_iota(jnp.int32, (256, width), 0).astype(F32).astype(BF16)
    return jnp.where(iota == jnp.broadcast_to(low.astype(BF16), (256, width)), 1.0, 0.0).astype(BF16)


def synth_kernel(coef_ref, az_ref, route_ref, out_ref, tr_ref):
    rows = az_ref.shape[1]
    tr_ref[...] = jnp.zeros(tr_ref.shape, BF16)
    for blk in range(rows // 128):
        sl = slice(blk * 128, blk * 128 + 128)
        phi = az_ref[:, sl]
        c1 = jnp.cos(phi)
        s1 = jnp.sin(phi)
        acc = [coef_ref[0, :, sl]] * 8
        cm, sm = c1, s1
        for m in range(1, 9):
            cc = coef_ref[m, :, sl]
            cs = coef_ref[8 + m, :, sl]
            for a in range(8):
                acc[a] = acc[a] + cc * cm[a : a + 1, :] + cs * sm[a : a + 1, :]
            cm, sm = cm * c1 - sm * s1, sm * c1 + cm * s1
        stack = jnp.concatenate([acc[a] for a in (0, 2, 4, 6, 1, 3, 5, 7)], axis=0)
        hi, lo = split2(stack)
        tr_ref[0:96, sl] = hi
        tr_ref[128:224, sl] = lo
    lane = lax.broadcasted_iota(jnp.int32, (128, rows), 1)
    for c in range(12):
        pick = jnp.where(route_ref[:, c : c + 1] == lane, 1.0, 0.0).astype(BF16)
        res = lax.dot_general(
            pick, tr_ref[...], (((1,), (1,)), ((), ())), preferred_element_type=F32
        )
        out_ref[pl.ds(c, 128, stride=16), :] = res[:, :128] + res[:, 128:]


def pick_kernel(got_ref, fp_ref, out_ref, tab_ref, h_ref, lo_ref):
    for c in range(12):
        blk = got_ref[pl.ds(c, 128, stride=16), :].T
        hi, lo = split2(halves(blk[0:48], blk[48:96]))
        tab_ref[c * 48 : c * 48 + 48, 0:256] = hi
        tab_ref[c * 48 : c * 48 + 48, 256:512] = lo
    p = halves(fp_ref[0:64, :], fp_ref[64:128, :])
    pf = p.astype(F32)
    a = ((pf + 0.5) * (1.0 / 1536.0)).astype(jnp.int32)
    n = p - a * 1536
    s = ((n.astype(F32) + 0.5) * (1.0 / 12.0)).astype(jnp.int32)
    c = n - s * 12
    h_ref[...] = jnp.where(p >= 12288, 1000, c * 4 + lax.shift_right_logical(a, 1))
    lo_ref[...] = ((jnp.bitwise_and(a, 1) * 128) + s).astype(F32)
    width = 512
    sub12 = lax.broadcasted_iota(jnp.int32, (48, width), 0) // 12
    lane = lax.broadcasted_iota(jnp.int32, (8, 128), 1)

    def body(g, carry):
        oh = one_hot(lanes_of_rows(lo_ref, 4 * g, 4), width)
        res = jnp.dot(
            tab_ref[...], jnp.concatenate([oh, oh], axis=0), preferred_element_type=F32
        )
        hb = jnp.broadcast_to(lanes_of_rows(h_ref, 4 * g, 4), (48, width)) - sub12
        acc = jnp.zeros((48, width), F32)
        for q in range(12):
            acc = jnp.where(hb == 4 * q, res[48 * q : 48 * q + 48], acc)
        acc = acc[0:24] + acc[24:48]
        acc = acc[0:12] + acc[12:24]
        x = acc[0:8]
        y = jnp.concatenate([acc[8:12], acc[8:12]], axis=0)
        for q in range(4):
            xq = x[:, 128 * q : 128 * q + 128]
            yq = y[:, 128 * q : 128 * q + 128]
            row = (4 * g + q) * 8
            out_ref[pl.ds(pl.multiple_of(row, 8), 8), :] = jnp.where(
                lane < 64, xq, pltpu.roll(yq, 64, 1)
            )
            out_ref[pl.ds(pl.multiple_of(row + 512, 8), 8), :] = jnp.where(
                lane < 64, pltpu.roll(xq, 64, 1), yq
            )
        return carry

    lax.fori_loop(0, 16, body, 0)


X0, X4, Y0, Y4, Z0, Z4 = range(6)


def face_pieces(face):
    if face == X0:
        return [(0, 25, 1, 0)]
    if face == X4:
        return [(100, 25, 1, 0)]
    if face == Y0:
        return [(25 * i, 5, 1, 5 * i) for i in range(5)]
    if face == Y4:
        return [(25 * i + 20, 5, 1, 5 * i) for i in range(5)]
    if face == Z0:
        return [(0, 25, 5, 0)]
    return [(4, 25, 5, 0)]


def rows_at(start, count, stride):
    return pl.ds(start, count, stride=stride) if stride > 1 else pl.ds(start, count)


def take_face(f_ref, face, out_ref):
    for c in range(3):
        for start, count, stride, dst in face_pieces(face):
            out_ref[pl.ds(c * 32 + dst, count), :] = f_ref[rows_at(c * 128 + start, count, stride), :]


def add_face(f_ref, face, vals):
    for c in range(3):
        for start, count, stride, dst in face_pieces(face):
            at = rows_at(c * 128 + start, count, stride)
            f_ref[at, :] = f_ref[at, :] + vals[c * 32 + dst : c * 32 + dst + count, :]


def dot3(x, mat):
    hi = x.astype(BF16)
    rest = x - hi.astype(F32)
    mid, low = split2(rest)
    parts = jnp.concatenate([hi, mid, low], axis=0)
    n = x.shape[0]
    res = jnp.dot(parts, mat, preferred_element_type=F32)
    return res[0:n] + res[n : 2 * n] + res[2 * n : 3 * n]


def column(row):
    return jnp.broadcast_to(row, (128, 128)).T


def match(col, row, good):
    return jnp.where((col == row) & good, 1.0, 0.0).astype(BF16)


def main_kernel(
    n_slab,
    n_sec,
    arr_ref,
    fn_ref,
    disp_ref,
    veloc_ref,
    mem_ref,
    conn_ref,
    xs_ref,
    ys_ref,
    absorb_ref,
    damp_ref,
    mod_ref,
    mass_ref,
    grad_ref,
    gradt_ref,
    cube_ref,
    outd_ref,
    outv_ref,
    conn_s,
    sh_s,
    tab0_s,
    tabm_s,
    tabi_s,
    st_s,
    ie_s,
    m_s,
    dep_s,
    val_s,
    f_s,
    fa_s,
    fb_s,
    w_s,
    acc_s,
    mat_s,
    kown_s,
    kgot_s,
    send_s,
    recv_s,
    ksem_send,
    ksem_recv,
    sem_send,
    sem_recv,
):
    slab = lax.axis_index("slab")
    sec = lax.axis_index("sec")
    nodes = disp_ref.shape[1]
    groups = -(-nodes // 256)
    nxt_x = lax.rem(slab + 1, n_slab)
    prv_x = lax.rem(slab + n_slab - 1, n_slab)
    nxt_y = lax.rem(sec + 1, n_sec)
    prv_y = lax.rem(sec + n_sec - 1, n_sec)
    targets = [(prv_x, sec), (nxt_x, sec), (slab, prv_y), (slab, nxt_y)]

    barrier = pltpu.get_barrier_semaphore()
    for dev in targets:
        pl.semaphore_signal(barrier, inc=1, device_id=dev, device_id_type=MESH)

    conn_s[...] = jnp.full(conn_s.shape, 1 << 20, jnp.int32)
    conn_s[0:125, :] = conn_ref[...]
    sh_s[...] = jnp.full(sh_s.shape, -1, jnp.int32)
    sh_s[0:2, 0 : xs_ref.shape[1]] = xs_ref[...]
    sh_s[2:4, 0 : ys_ref.shape[1]] = ys_ref[...]

    kown_s[...] = jnp.zeros(kown_s.shape, F32)
    for r, point in ((0, 12), (1, 112), (2, 52), (3, 72)):
        centre = conn_s[point : point + 1, :]
        best = jnp.zeros((128, 128), jnp.int32)
        for b in range(5):
            col = column(sh_s[r : r + 1, b * 128 : b * 128 + 128])
            slot = lax.broadcasted_iota(jnp.int32, (128, 128), 0) + (b * 128 + 1)
            best = jnp.maximum(best, jnp.where(col == centre, slot, 0))
        kown_s[r : r + 1, :] = jnp.max(best, axis=0, keepdims=True).astype(F32)

    pl.semaphore_wait(barrier, 4)
    kcopies = []
    for d, dev in enumerate(targets):
        copy = pltpu.make_async_remote_copy(
            src_ref=kown_s,
            dst_ref=kgot_s.at[d ^ 1],
            send_sem=ksem_send.at[d],
            recv_sem=ksem_recv.at[d ^ 1],
            device_id=dev,
            device_id_type=MESH,
        )
        copy.start()
        kcopies.append(copy)

    tab0_s[...] = jnp.zeros(tab0_s.shape, F32)
    tab0_s[0:3, 0:nodes] = disp_ref[...]
    tab0_s[3:6, 0:nodes] = veloc_ref[...]
    tab0_s[6:7, 0:nodes] = mass_ref[...]
    for h2 in range(groups // 2):
        two = jnp.concatenate(
            [tab0_s[:, h2 * 512 : h2 * 512 + 256], tab0_s[:, h2 * 512 + 256 : h2 * 512 + 512]], axis=0
        )
        hi, lo = split2(two)
        tabm_s[h2 * 16 : h2 * 16 + 16, 0:256] = hi
        tabm_s[h2 * 16 : h2 * 16 + 16, 256:512] = lo

    width = 512

    def pick_state(g, carry):
        idx = lanes_of_rows(conn_s, 4 * g, 4)
        oh = one_hot(jnp.bitwise_and(idx, 255).astype(F32), width)
        res = jnp.dot(
            tabm_s[...], jnp.concatenate([oh, oh], axis=0), preferred_element_type=F32
        )
        hb = jnp.broadcast_to(lax.shift_right_logical(idx, 8), (8, width))
        acc = jnp.zeros((8, width), F32)
        for h in range(groups):
            acc = jnp.where(hb == h, res[8 * h : 8 * h + 8], acc)
        for q in range(4):
            st_s[pl.ds(4 * g + q, 8, stride=128), :] = acc[:, 128 * q : 128 * q + 128]
        return carry

    lax.fori_loop(0, 32, pick_state, 0)

    sub12 = lax.broadcasted_iota(jnp.int32, (48, 256), 0) // 12
    lane = lax.broadcasted_iota(jnp.int32, (8, 128), 1)
    dep_s[...] = jnp.zeros(dep_s.shape, F32)

    def deposit(g, carry):
        vals = []
        idxs = []
        for q in range(2):
            row = (2 * g + q) * 8
            c0 = arr_ref[pl.ds(pl.multiple_of(row, 8), 8), :]
            c1 = arr_ref[pl.ds(pl.multiple_of(row + 512, 8), 8), :]
            x = jnp.where(lane < 64, c0, pltpu.roll(c1, 64, 1))
            y = jnp.where(lane < 64, pltpu.roll(c0, 64, 1), c1)
            v12 = jnp.concatenate([x, y[0:4]], axis=0)
            v24 = jnp.concatenate([v12, v12], axis=0)
            vals.append(jnp.concatenate([v24, v24], axis=0))
            idxs.append(halves(fn_ref[pl.ds(2 * g + q, 1), :], fn_ref[pl.ds(2 * g + q + 64, 1), :]))
        val = jnp.concatenate(vals, axis=1)
        idx = jnp.concatenate(idxs, axis=1)
        idx = jnp.where(idx >= nodes, 1 << 20, idx)
        vhi, vlo = split2(val)
        oh = one_hot(jnp.bitwise_and(idx, 255).astype(F32), 256)
        high = jnp.minimum(lax.shift_right_logical(idx, 8), 200)
        hb = (jnp.broadcast_to(high, (48, 256)) - sub12).astype(F32).astype(BF16)
        zero = jnp.zeros((48, 256), BF16)
        lhs = []
        for q in range(10):
            mask = hb == jnp.asarray(4 * q, BF16)
            lhs.append(halves(jnp.where(mask, vhi, zero), jnp.where(mask, vlo, zero)))
        lhs = jnp.concatenate(lhs, axis=0)
        dep_s[...] += lax.dot_general(
            lhs, halves(oh, oh), (((1,), (1,)), ((), ())), preferred_element_type=F32
        )
        return carry

    lax.fori_loop(0, 32, deposit, 0)

    hi, lo = split2(dep_s[...])
    tabi_s[:, 0:256] = hi
    tabi_s[:, 256:512] = lo
    sub12w = lax.broadcasted_iota(jnp.int32, (48, width), 0) // 12

    def pick_inj(g, carry):
        idx = lanes_of_rows(conn_s, 4 * g, 4)
        oh = one_hot(jnp.bitwise_and(idx, 255).astype(F32), width)
        res = jnp.dot(
            tabi_s[...], jnp.concatenate([oh, oh], axis=0), preferred_element_type=F32
        )
        hb = jnp.broadcast_to(lax.shift_right_logical(idx, 8), (48, width)) - sub12w
        acc = jnp.zeros((48, width), F32)
        for q in range(10):
            acc = jnp.where(hb == 4 * q, res[48 * q : 48 * q + 48], acc)
        acc = acc[0:24] + acc[24:48]
        acc = acc[0:12] + acc[12:24]
        for q in range(4):
            part = acc[:, 128 * q : 128 * q + 128]
            ie_s[pl.ds(4 * g + q, 8, stride=128), :] = part[0:8]
            ie_s[pl.ds(8 * 128 + 4 * g + q, 4, stride=128), :] = part[8:12]
        return carry

    lax.fori_loop(0, 32, pick_inj, 0)

    for copy in kcopies:
        copy.wait()
    true = jnp.full((128, 128), True)
    for d, (low_point, high_point) in enumerate(((12, 112), (52, 72), (60, 64))):
        low = conn_s[low_point : low_point + 1, :]
        high = conn_s[high_point : high_point + 1, :]
        mat_s[2 * d, 0:128, :] = match(column(high), low, true)
        mat_s[2 * d + 1, 0:128, :] = match(column(low), high, true)
        if d < 2:
            pos, count = ((slab, n_slab), (sec, n_sec))[d]
            low_k = kown_s[2 * d : 2 * d + 1, :]
            high_k = kown_s[2 * d + 1 : 2 * d + 2, :]
            from_prev = column(kgot_s[2 * d, 2 * d + 1 : 2 * d + 2, :])
            from_next = column(kgot_s[2 * d + 1, 2 * d : 2 * d + 1, :])
            mat_s[2 * d, 128:256, :] = match(from_prev, low_k, (low_k > 0.5) & (pos > 0))
            mat_s[2 * d + 1, 128:256, :] = match(
                from_next, high_k, (high_k > 0.5) & (pos < count - 1)
            )

    def local_sum(d):
        take_face(f_s, 2 * d, fa_s)
        take_face(f_s, 2 * d + 1, fb_s)
        into_low = dot3(fb_s[...], mat_s[2 * d, 0:128, :])
        into_high = dot3(fa_s[...], mat_s[2 * d + 1, 0:128, :])
        add_face(f_s, 2 * d, into_low)
        add_face(f_s, 2 * d + 1, into_high)

    fa_s[...] = jnp.zeros(fa_s.shape, F32)
    fb_s[...] = jnp.zeros(fb_s.shape, F32)
    send_s[...] = jnp.zeros(send_s.shape, F32)
    f_s[...] = jnp.ones(f_s.shape, F32)
    for d in range(3):
        local_sum(d)
    w_s[...] = 1.0 / f_s[0:128, :]

    absorb = absorb_ref[...].astype(F32)
    retain = jnp.exp(-DT * damp_ref[...])
    m_s[...] = jnp.zeros(m_s.shape, F32)
    for d in range(3):
        for c in range(3):
            m_s[d * 128 : d * 128 + 125, c * 128 : c * 128 + 128] = mem_ref[3 * d + c]
    row = lax.broadcasted_iota(jnp.int32, (128, 128), 0)
    mass = st_s[768:896, :]
    st_s[896:1024, :] = jnp.where(row < 125, DT / jnp.where(row < 125, mass, 1.0), 0.0)
    acc_s[...] = jnp.zeros(acc_s.shape, F32)

    def step(n, carry):
        u = jnp.concatenate([st_s[c * 128 : c * 128 + 128, :] for c in range(3)], axis=1)
        g = jnp.dot(grad_ref[...], u, precision=HIGHEST, preferred_element_type=F32)
        wide = lambda x: jnp.concatenate([x, x, x], axis=1)
        ab, rt = wide(absorb), wide(retain)
        weight = wide(mod_ref[...] * cube_ref[...])
        weight = jnp.concatenate([weight, weight, weight], axis=0)
        mem = m_s[...]
        stress = weight * (g - ab * mem)
        m_s[...] = ab * (rt * mem + (1.0 - rt) * g)
        div = jnp.dot(gradt_ref[...], stress, precision=HIGHEST, preferred_element_type=F32)
        for c in range(3):
            at = slice(c * 128, c * 128 + 128)
            inj = ie_s[pl.ds(pl.multiple_of(n * 384 + c * 128, 128), 128), :]
            f_s[at, :] = w_s[...] * inj - div[:, at]
        for d in range(2):
            sends = []
            for side in range(2):
                part = 2 * d + side
                take_face(f_s, part, send_s.at[part])
            for side in range(2):
                part = 2 * d + side
                copy = pltpu.make_async_remote_copy(
                    src_ref=send_s.at[part],
                    dst_ref=recv_s.at[n, part ^ 1],
                    send_sem=sem_send.at[n, part],
                    recv_sem=sem_recv.at[n, part ^ 1],
                    device_id=targets[part],
                    device_id_type=MESH,
                )
                copy.start()
                sends.append(copy)
            into_low = dot3(send_s[2 * d + 1], mat_s[2 * d, 0:128, :])
            into_high = dot3(send_s[2 * d], mat_s[2 * d + 1, 0:128, :])
            for copy in sends:
                copy.wait()
            into_low += dot3(recv_s[n, 2 * d], mat_s[2 * d, 128:256, :])
            into_high += dot3(recv_s[n, 2 * d + 1], mat_s[2 * d + 1, 128:256, :])
            add_face(f_s, 2 * d, into_low)
            add_face(f_s, 2 * d + 1, into_high)
        local_sum(2)
        total = f_s[...]
        scale = st_s[896:1024, :]
        scale = jnp.concatenate([scale, scale, scale], axis=0)
        v = st_s[384:768, :] + total * scale
        st_s[384:768, :] = v
        st_s[0:384, :] = st_s[0:384, :] + DT * v
        w3 = jnp.concatenate([w_s[...], w_s[...], w_s[...]], axis=0)
        own = w3 * (total - ie_s[pl.ds(pl.multiple_of(n * 384, 128), 384), :])
        acc_s[0:384, :] = acc_s[0:384, :] + own
        acc_s[384:768, :] = acc_s[384:768, :] + (4 - n).astype(F32) * own
        return carry

    lax.fori_loop(0, 4, step, 0)

    val_s[...] = jnp.zeros(val_s.shape, F32)
    sub8 = lax.broadcasted_iota(jnp.int32, (16, width), 0) // 8

    def collect(g, carry):
        idx = lanes_of_rows(conn_s, 4 * g, 4)
        vals = []
        for q in range(4):
            six = acc_s[pl.ds(4 * g + q, 8, stride=128), :]
            vals.append(jnp.concatenate([six, six], axis=0))
        vhi, vlo = split2(jnp.concatenate(vals, axis=1))
        oh = one_hot(jnp.bitwise_and(idx, 255).astype(F32), width)
        high = jnp.minimum(lax.shift_right_logical(idx, 8), 200)
        hb = (jnp.broadcast_to(high, (16, width)) - sub8).astype(F32).astype(BF16)
        zero = jnp.zeros((16, width), BF16)
        lhs = []
        for q in range(groups // 2):
            mask = hb == jnp.asarray(2 * q, BF16)
            lhs.append(halves(jnp.where(mask, vhi, zero), jnp.where(mask, vlo, zero)))
        lhs = jnp.concatenate(lhs, axis=0)
        val_s[...] += lax.dot_general(
            lhs, halves(oh, oh), (((1,), (1,)), ((), ())), preferred_element_type=F32
        )
        return carry

    lax.fori_loop(0, 32, collect, 0)

    for h in range(groups):
        size = min(256, nodes - h * 256)
        at = slice(h * 256, h * 256 + size)
        lanes = slice(0, size)
        inv = DT / mass_ref[:, at]
        inj = [dep_s[12 * h + 3 * n : 12 * h + 3 * n + 3, lanes] for n in range(4)]
        vsum = inj[0] + inj[1] + inj[2] + inj[3] + val_s[8 * h : 8 * h + 3, lanes]
        usum = 4.0 * inj[0] + 3.0 * inj[1] + 2.0 * inj[2] + inj[3] + val_s[8 * h + 3 : 8 * h + 6, lanes]
        v0 = veloc_ref[:, at]
        outv_ref[:, at] = v0 + inv * vsum
        outd_ref[:, at] = disp_ref[:, at] + (4.0 * DT) * v0 + (DT * inv) * usum


def local(n_slab, n_sec):
    grad, gradt, cube = gll_tables()
    params = pltpu.CompilerParams(vmem_limit_bytes=VMEM_LIMIT)
    vmem = pl.BlockSpec(memory_space=pltpu.VMEM)

    def run(
        coefficients,
        azimuths,
        route_rows,
        face_points,
        face_nodes,
        disp_start,
        veloc_start,
        memory_start,
        connectivity,
        x_shared,
        y_shared,
        absorbing,
        damping,
        modulus,
        masses,
    ):
        devices = n_slab * n_sec
        rows = azimuths.shape[1]
        nodes = disp_start.shape[1]
        payload = pl.pallas_call(
            synth_kernel,
            out_shape=jax.ShapeDtypeStruct((devices * 16, 128), F32),
            in_specs=[vmem] * 3,
            out_specs=vmem,
            scratch_shapes=[pltpu.VMEM((256, rows), BF16)],
            compiler_params=params,
            name="synthesis",
        )(coefficients, azimuths, route_rows.reshape(devices, 12))
        got = lax.all_to_all(
            payload.reshape(devices, 16, 128), ("slab", "sec"), split_axis=0, concat_axis=0, tiled=True
        )
        sent = pl.pallas_call(
            pick_kernel,
            out_shape=jax.ShapeDtypeStruct((devices * 8, 128), F32),
            in_specs=[vmem] * 2,
            out_specs=vmem,
            scratch_shapes=[
                pltpu.VMEM((576, 512), BF16),
                pltpu.VMEM((64, 128), jnp.int32),
                pltpu.VMEM((64, 128), F32),
            ],
            compiler_params=params,
            name="points",
        )(got.reshape(devices * 16, 128), face_points.reshape(devices, 64))
        arrived = lax.all_to_all(
            sent.reshape(devices, 8, 128), ("slab", "sec"), split_axis=0, concat_axis=0, tiled=True
        )
        groups = -(-nodes // 256)
        dma = pltpu.SemaphoreType.DMA
        return pl.pallas_call(
            lambda *refs: main_kernel(n_slab, n_sec, *refs),
            out_shape=(
                jax.ShapeDtypeStruct((3, nodes), F32),
                jax.ShapeDtypeStruct((3, nodes), F32),
            ),
            in_specs=[vmem] * 15,
            out_specs=(vmem, vmem),
            scratch_shapes=[
                pltpu.VMEM((128, 128), jnp.int32),
                pltpu.VMEM((8, 640), jnp.int32),
                pltpu.VMEM((8, groups * 256), F32),
                pltpu.VMEM((groups * 8, 512), BF16),
                pltpu.VMEM((480, 512), BF16),
                pltpu.VMEM((1024, 128), F32),
                pltpu.VMEM((1536, 128), F32),
                pltpu.VMEM((384, 384), F32),
                pltpu.VMEM((480, 256), F32),
                pltpu.VMEM((groups * 8, 256), F32),
                pltpu.VMEM((384, 128), F32),
                pltpu.VMEM((96, 128), F32),
                pltpu.VMEM((96, 128), F32),
                pltpu.VMEM((128, 128), F32),
                pltpu.VMEM((1024, 128), F32),
                pltpu.VMEM((6, 256, 128), BF16),
                pltpu.VMEM((8, 128), F32),
                pltpu.VMEM((4, 8, 128), F32),
                pltpu.VMEM((4, 96, 128), F32),
                pltpu.VMEM((4, 4, 96, 128), F32),
                dma((4,)),
                dma((4,)),
                dma((4, 4)),
                dma((4, 4)),
            ],
            compiler_params=pltpu.CompilerParams(
                vmem_limit_bytes=VMEM_LIMIT, collective_id=0, has_side_effects=True
            ),
            name="slab_steps",
        )(
            arrived.reshape(devices * 8, 128),
            face_nodes.reshape(devices, 64),
            disp_start,
            veloc_start,
            memory_start,
            connectivity,
            x_shared,
            y_shared,
            absorbing.reshape(1, -1),
            damping.reshape(1, -1),
            modulus.reshape(1, -1),
            masses.reshape(1, -1),
            grad,
            gradt,
            cube,
        )

    return run


def solution(mesh):
    both = ("slab", "sec")
    return jax.shard_map(
        local(mesh.shape["slab"], mesh.shape["sec"]),
        mesh=mesh,
        in_specs=(
            P(None, None, both),
            P(None, both),
            P(both, None, None),
            P(both, None, None),
            P(both, None, None),
            P(None, both),
            P(None, both),
            P(None, None, both),
            P(None, both),
            P(None, both),
            P(None, both),
            P(both),
            P(both),
            P(both),
            P(both),
        ),
        out_specs=(P(None, both), P(None, both)),
        check_vma=False,
    )
```

```python
import math

import jax
import jax.numpy as jnp
import numpy as np
from jax import lax
from jax.experimental import pallas as pl
from jax.experimental.pallas import tpu as pltpu
from jax.sharding import PartitionSpec as P

F32 = jnp.float32
BF16 = jnp.bfloat16
HIGHEST = lax.Precision.HIGHEST
MESH = pl.DeviceIdType.MESH
DT = 0.1
VMEM_LIMIT = 56 * 2**20


def gll_tables():
    points = np.array([-1.0, -math.sqrt(3.0 / 7.0), 0.0, math.sqrt(3.0 / 7.0), 1.0])
    weights = np.array([0.1, 49.0 / 90.0, 32.0 / 45.0, 49.0 / 90.0, 0.1])
    products = np.array(
        [np.prod([points[r] - points[c] for c in range(5) if c != r]) for r in range(5)]
    )
    derivative = np.zeros((5, 5))
    for r in range(5):
        for c in range(5):
            if r != c:
                derivative[r, c] = products[r] / (products[c] * (points[r] - points[c]))
        derivative[r, r] = -derivative[r].sum()
    cube = weights[:, None, None] * weights[None, :, None] * weights[None, None, :]
    eye = np.eye(5)
    grad = np.zeros((3, 128, 128))
    grad[0, :125, :125] = np.kron(derivative, np.kron(eye, eye))
    grad[1, :125, :125] = np.kron(eye, np.kron(derivative, eye))
    grad[2, :125, :125] = np.kron(eye, np.kron(eye, derivative))
    grad = grad.reshape(384, 128).astype(np.float32)
    cube128 = np.zeros((128, 128), np.float32)
    cube128[:125] = cube.reshape(125, 1)
    return grad, np.ascontiguousarray(grad.T), cube128


def split2(x):
    hi = x.astype(BF16)
    return hi, (x - hi.astype(F32)).astype(BF16)


def halves(low, high):
    return jnp.concatenate([low, high], axis=1)


def lanes_of_rows(ref, start, count):
    return jnp.concatenate([ref[pl.ds(start + q, 1), :] for q in range(count)], axis=1)


def one_hot(low, width):
    iota = lax.broadcasted_iota(jnp.int32, (256, width), 0).astype(F32).astype(BF16)
    hit = iota == jnp.broadcast_to(low.astype(F32).astype(BF16), (256, width))
    return jnp.where(hit, jnp.ones((256, width), BF16), jnp.zeros((256, width), BF16))


X0, X4, Y0, Y4, Z0, Z4 = range(6)


def face_pieces(face):
    if face == X0:
        return [(0, 25, 1, 0)]
    if face == X4:
        return [(100, 25, 1, 0)]
    if face == Y0:
        return [(25 * i, 5, 1, 5 * i) for i in range(5)]
    if face == Y4:
        return [(25 * i + 20, 5, 1, 5 * i) for i in range(5)]
    if face == Z0:
        return [(0, 25, 5, 0)]
    return [(4, 25, 5, 0)]


def rows_at(start, count, stride):
    return pl.ds(start, count, stride=stride) if stride > 1 else pl.ds(start, count)


def take_face(f_ref, face, out_ref):
    for c in range(3):
        for start, count, stride, dst in face_pieces(face):
            out_ref[pl.ds(c * 32 + dst, count), :] = f_ref[rows_at(c * 128 + start, count, stride), :]


def add_face(f_ref, face, vals):
    for c in range(3):
        for start, count, stride, dst in face_pieces(face):
            at = rows_at(c * 128 + start, count, stride)
            f_ref[at, :] = f_ref[at, :] + vals[c * 32 + dst : c * 32 + dst + count, :]


def dot3(x, mat):
    hi = x.astype(BF16)
    rest = x - hi.astype(F32)
    mid, low = split2(rest)
    parts = jnp.concatenate([hi, mid, low], axis=0)
    n = x.shape[0]
    res = jnp.dot(parts, mat, preferred_element_type=F32)
    return res[0:n] + res[n : 2 * n] + res[2 * n : 3 * n]


def column(row):
    return jnp.broadcast_to(row, (128, 128)).T


def match(col, row, good):
    return jnp.where((col == row) & good, 1.0, 0.0).astype(BF16)


def synthesize(coef_ref, az_ref, route_ref, tr_ref, send_ref):
    rows = az_ref.shape[1]
    tr_ref[...] = jnp.zeros(tr_ref.shape, BF16)
    for blk in range(rows // 128):
        sl = slice(blk * 128, blk * 128 + 128)
        phi = az_ref[:, sl]
        c1 = jnp.cos(phi)
        s1 = jnp.sin(phi)
        acc = [coef_ref[0, :, sl]] * 8
        cm, sm = c1, s1
        for m in range(1, 9):
            cc = coef_ref[m, :, sl]
            cs = coef_ref[8 + m, :, sl]
            for a in range(8):
                acc[a] = acc[a] + cc * cm[a : a + 1, :] + cs * sm[a : a + 1, :]
            cm, sm = cm * c1 - sm * s1, sm * c1 + cm * s1
        stack = jnp.concatenate([acc[a] for a in (0, 2, 4, 6, 1, 3, 5, 7)], axis=0)
        hi, lo = split2(stack)
        tr_ref[0:96, sl] = hi
        tr_ref[128:224, sl] = lo
    lane = lax.broadcasted_iota(jnp.int32, (128, rows), 1)
    lane1 = lax.broadcasted_iota(jnp.int32, (128, 128), 1)
    for quad in range(3):
        got = []
        for c in range(4 * quad, 4 * quad + 4):
            col = jnp.concatenate([column(route_ref[c])] * (rows // 128), axis=1)
            pick = jnp.where(col == lane, 1.0, 0.0).astype(BF16)
            res = lax.dot_general(
                pick, tr_ref[...], (((1,), (1,)), ((), ())), preferred_element_type=F32
            )
            got.append(res[:, :128] + res[:, 128:])
        b1 = pltpu.roll(got[1], 96, 1)
        b2 = pltpu.roll(got[2], 64, 1)
        b3 = pltpu.roll(got[3], 32, 1)
        send_ref[pl.ds(3 * quad, 128, stride=16), :] = jnp.where(lane1 < 96, got[0], b1)
        send_ref[pl.ds(3 * quad + 1, 128, stride=16), :] = jnp.where(lane1 < 64, b1, b2)
        send_ref[pl.ds(3 * quad + 2, 128, stride=16), :] = jnp.where(lane1 < 32, b2, b3)


def paired(ref):
    two = jnp.concatenate([ref[...], ref[...]], axis=0).T
    lane = lax.broadcasted_iota(jnp.int32, (64, 128), 1)
    return jnp.where(lane < 64, two[0:64], two[64:128])


def mega_kernel(
    n_slab,
    n_sec,
    coef_ref,
    az_ref,
    route_ref,
    fp_ref,
    fn_ref,
    disp_ref,
    veloc_ref,
    mem_ref,
    conn_ref,
    xs_ref,
    ys_ref,
    absorb_ref,
    damp_ref,
    mod_ref,
    mass_ref,
    grad_ref,
    gradt_ref,
    cube_ref,
    outd_ref,
    outv_ref,
    tr_s,
    rows_send,
    rows_got,
    pts_send,
    pts_got,
    tabp_s,
    h_s,
    lo_s,
    fn_s,
    conn_s,
    sh_s,
    tab0_s,
    tabm_s,
    tabi_s,
    st_s,
    ie_s,
    m_s,
    dep_s,
    val_s,
    f_s,
    fa_s,
    fb_s,
    w_s,
    acc_s,
    mat_s,
    kown_s,
    kgot_s,
    send_s,
    recv_s,
    ksem_send,
    ksem_recv,
    sem_send,
    sem_recv,
    rsem_send,
    rsem_recv,
    psem_send,
    psem_recv,
):
    slab = lax.axis_index("slab")
    sec = lax.axis_index("sec")
    me = slab * n_sec + sec
    devices = n_slab * n_sec
    nodes = disp_ref.shape[1]
    groups = -(-nodes // 256)
    nxt_x = lax.rem(slab + 1, n_slab)
    prv_x = lax.rem(slab + n_slab - 1, n_slab)
    nxt_y = lax.rem(sec + 1, n_sec)
    prv_y = lax.rem(sec + n_sec - 1, n_sec)
    targets = [(prv_x, sec), (nxt_x, sec), (slab, prv_y), (slab, nxt_y)]

    def place(d):
        return (d // n_sec, lax.rem(d, n_sec))

    barrier = pltpu.get_barrier_semaphore()

    def greet(j, carry):
        d = lax.rem(me + j, devices)
        pl.semaphore_signal(barrier, inc=1, device_id=place(d), device_id_type=MESH)
        return carry

    lax.fori_loop(1, devices, greet, 0)

    synthesize(coef_ref, az_ref, route_ref, tr_s, rows_send)

    pl.semaphore_wait(barrier, devices - 1)

    def send_rows(j, carry):
        d = lax.rem(me + j, devices)
        pltpu.make_async_remote_copy(
            src_ref=rows_send.at[pl.ds(d * 16, 9)],
            dst_ref=rows_got.at[pl.ds(me * 16, 9)],
            send_sem=rsem_send,
            recv_sem=rsem_recv,
            device_id=place(d),
            device_id_type=MESH,
        ).start()
        return carry

    lax.fori_loop(1, devices, send_rows, 0)
    own = pl.ds(pl.multiple_of(me * 16, 16), 16)
    rows_got[own, :] = rows_send[own, :]

    conn_s[...] = jnp.full(conn_s.shape, 1 << 20, jnp.int32)
    conn_s[0:125, :] = conn_ref[...]
    sh_s[...] = jnp.full(sh_s.shape, -1, jnp.int32)
    sh_s[0:2, 0 : xs_ref.shape[1]] = xs_ref[...]
    sh_s[2:4, 0 : ys_ref.shape[1]] = ys_ref[...]

    kown_s[...] = jnp.zeros(kown_s.shape, F32)
    for r, point in ((0, 12), (1, 112), (2, 52), (3, 72)):
        centre = conn_s[point : point + 1, :]
        best = jnp.zeros((128, 128), jnp.int32)
        for b in range(5):
            col = column(sh_s[r : r + 1, b * 128 : b * 128 + 128])
            slot = lax.broadcasted_iota(jnp.int32, (128, 128), 0) + (b * 128 + 1)
            best = jnp.maximum(best, jnp.where(col == centre, slot, 0))
        kown_s[r : r + 1, :] = jnp.max(best, axis=0, keepdims=True).astype(F32)
    kcopies = []
    for d, dev in enumerate(targets):
        copy = pltpu.make_async_remote_copy(
            src_ref=kown_s,
            dst_ref=kgot_s.at[d ^ 1],
            send_sem=ksem_send.at[d],
            recv_sem=ksem_recv.at[d ^ 1],
            device_id=dev,
            device_id_type=MESH,
        )
        copy.start()
        kcopies.append(copy)

    tab0_s[...] = jnp.zeros(tab0_s.shape, F32)
    tab0_s[0:3, 0:nodes] = disp_ref[...]
    tab0_s[3:6, 0:nodes] = veloc_ref[...]
    for h in range(nodes // 128):
        tab0_s[6:7, h * 128 : h * 128 + 128] = mass_ref[h : h + 1, :]
    for h2 in range(groups // 2):
        two = jnp.concatenate(
            [tab0_s[:, h2 * 512 : h2 * 512 + 256], tab0_s[:, h2 * 512 + 256 : h2 * 512 + 512]], axis=0
        )
        hi, lo = split2(two)
        tabm_s[h2 * 16 : h2 * 16 + 16, 0:256] = hi
        tabm_s[h2 * 16 : h2 * 16 + 16, 256:512] = lo

    width = 512

    def pick_state(g, carry):
        idx = lanes_of_rows(conn_s, 4 * g, 4)
        oh = one_hot(jnp.bitwise_and(idx, 255), width)
        res = jnp.dot(
            tabm_s[...], jnp.concatenate([oh, oh], axis=0), preferred_element_type=F32
        )
        hb = jnp.broadcast_to(lax.shift_right_logical(idx, 8), (8, width))
        acc = jnp.zeros((8, width), F32)
        for h in range(groups):
            acc = jnp.where(hb == h, res[8 * h : 8 * h + 8], acc)
        for q in range(4):
            st_s[pl.ds(4 * g + q, 8, stride=128), :] = acc[:, 128 * q : 128 * q + 128]
        return carry

    lax.fori_loop(0, 32, pick_state, 0, unroll=2)

    absorb = absorb_ref[...].astype(F32)
    retain = jnp.exp(-DT * damp_ref[...])
    m_s[...] = jnp.zeros(m_s.shape, F32)
    for d in range(3):
        for c in range(3):
            m_s[d * 128 : d * 128 + 125, c * 128 : c * 128 + 128] = mem_ref[3 * d + c]
    row = lax.broadcasted_iota(jnp.int32, (128, 128), 0)
    mass = st_s[768:896, :]
    st_s[896:1024, :] = jnp.where(row < 125, DT / jnp.where(row < 125, mass, 1.0), 0.0)
    acc_s[...] = jnp.zeros(acc_s.shape, F32)

    for copy in kcopies:
        copy.wait()
    true = jnp.full((128, 128), True)
    for d, (low_point, high_point) in enumerate(((12, 112), (52, 72), (60, 64))):
        low = conn_s[low_point : low_point + 1, :]
        high = conn_s[high_point : high_point + 1, :]
        mat_s[2 * d, 0:128, :] = match(column(high), low, true)
        mat_s[2 * d + 1, 0:128, :] = match(column(low), high, true)
        if d < 2:
            pos, count = ((slab, n_slab), (sec, n_sec))[d]
            low_k = kown_s[2 * d : 2 * d + 1, :]
            high_k = kown_s[2 * d + 1 : 2 * d + 2, :]
            from_prev = column(kgot_s[2 * d, 2 * d + 1 : 2 * d + 2, :])
            from_next = column(kgot_s[2 * d + 1, 2 * d : 2 * d + 1, :])
            mat_s[2 * d, 128:256, :] = match(from_prev, low_k, (low_k > 0.5) & (pos > 0))
            mat_s[2 * d + 1, 128:256, :] = match(
                from_next, high_k, (high_k > 0.5) & (pos < count - 1)
            )

    def local_sum(d):
        take_face(f_s, 2 * d, fa_s)
        take_face(f_s, 2 * d + 1, fb_s)
        into_low = dot3(fb_s[...], mat_s[2 * d, 0:128, :])
        into_high = dot3(fa_s[...], mat_s[2 * d + 1, 0:128, :])
        add_face(f_s, 2 * d, into_low)
        add_face(f_s, 2 * d + 1, into_high)

    fa_s[...] = jnp.zeros(fa_s.shape, F32)
    fb_s[...] = jnp.zeros(fb_s.shape, F32)
    send_s[...] = jnp.zeros(send_s.shape, F32)
    f_s[...] = jnp.ones(f_s.shape, F32)
    for d in range(3):
        local_sum(d)
    w_s[...] = 1.0 / f_s[0:128, :]

    def element_force():
        u = jnp.concatenate([st_s[c * 128 : c * 128 + 128, :] for c in range(3)], axis=1)
        g = jnp.dot(grad_ref[...], u, precision=HIGHEST, preferred_element_type=F32)
        wide = lambda x: jnp.concatenate([x, x, x], axis=1)
        ab, rt = wide(absorb), wide(retain)
        weight = wide(mod_ref[...] * cube_ref[...])
        weight = jnp.concatenate([weight, weight, weight], axis=0)
        mem = m_s[...]
        stress = weight * (g - ab * mem)
        m_s[...] = ab * (rt * mem + (1.0 - rt) * g)
        div = jnp.dot(gradt_ref[...], stress, precision=HIGHEST, preferred_element_type=F32)
        for c in range(3):
            f_s[c * 128 : c * 128 + 128, :] = -div[:, c * 128 : c * 128 + 128]

    element_force()

    p = paired(fp_ref)
    pf = p.astype(F32)
    a = ((pf + 0.5) * (1.0 / 1536.0)).astype(jnp.int32)
    n = p - a * 1536
    s = ((n.astype(F32) + 0.5) * (1.0 / 12.0)).astype(jnp.int32)
    c = n - s * 12
    h_s[...] = jnp.where(p >= 12288, 1000, c * 4 + lax.shift_right_logical(a, 1))
    lo_s[...] = jnp.bitwise_and(a, 1) * 128 + s
    fn_s[...] = paired(fn_ref)

    many = pl.ds(0, (devices - 1) * 9)
    pltpu.make_async_copy(rows_send.at[many], rows_got.at[many], rsem_recv).wait()
    blocks = [rows_got[pl.ds(j, 128, stride=16), :].T for j in range(9)]
    blocks = jnp.concatenate(blocks, axis=0)
    for c in range(12):
        base = c * 96
        hi, lo = split2(halves(blocks[base : base + 48], blocks[base + 48 : base + 96]))
        tabp_s[c * 48 : c * 48 + 48, 0:256] = hi
        tabp_s[c * 48 : c * 48 + 48, 256:512] = lo
    sub12 = lax.broadcasted_iota(jnp.int32, (48, width), 0) // 12
    lane = lax.broadcasted_iota(jnp.int32, (8, 128), 1)

    def send_points(d):
        @pl.when(d != me)
        def _():
            pltpu.make_async_remote_copy(
                src_ref=pts_send.at[pl.ds(d * 8, 8)],
                dst_ref=pts_got.at[pl.ds(me * 8, 8)],
                send_sem=psem_send,
                recv_sem=psem_recv,
                device_id=place(d),
                device_id_type=MESH,
            ).start()

    def pick_points(k, carry):
        g = lax.rem(k + me, 16)
        oh = one_hot(lanes_of_rows(lo_s, 4 * g, 4), width)
        res = jnp.dot(
            tabp_s[...], jnp.concatenate([oh, oh], axis=0), preferred_element_type=F32
        )
        hb = jnp.broadcast_to(lanes_of_rows(h_s, 4 * g, 4), (48, width)) - sub12
        acc = jnp.zeros((48, width), F32)
        for q in range(12):
            acc = jnp.where(hb == 4 * q, res[48 * q : 48 * q + 48], acc)
        acc = acc[0:24] + acc[24:48]
        acc = acc[0:12] + acc[12:24]
        x = acc[0:8]
        y = jnp.concatenate([acc[8:12], acc[8:12]], axis=0)
        for q in range(4):
            xq = x[:, 128 * q : 128 * q + 128]
            yq = y[:, 128 * q : 128 * q + 128]
            r = (4 * g + q) * 8
            pts_send[pl.ds(pl.multiple_of(r, 8), 8), :] = jnp.where(lane < 64, xq, pltpu.roll(yq, 64, 1))
            pts_send[pl.ds(pl.multiple_of(r + 512, 8), 8), :] = jnp.where(
                lane < 64, pltpu.roll(xq, 64, 1), yq
            )
        for q in range(4):
            send_points(4 * g + q)
            send_points(4 * g + q + 64)
        return carry

    lax.fori_loop(0, 16, pick_points, 0)
    own = pl.ds(pl.multiple_of(me * 8, 8), 8)
    pts_got[own, :] = pts_send[own, :]
    many = pl.ds(0, (devices - 1) * 8)
    pltpu.make_async_copy(pts_send.at[many], pts_got.at[many], psem_recv).wait()

    dep_s[...] = jnp.zeros(dep_s.shape, F32)

    def deposit(g, carry):
        vals = []
        for q in range(4):
            r = (4 * g + q) * 8
            c0 = pts_got[pl.ds(pl.multiple_of(r, 8), 8), :]
            c1 = pts_got[pl.ds(pl.multiple_of(r + 512, 8), 8), :]
            x = jnp.where(lane < 64, c0, pltpu.roll(c1, 64, 1))
            y = jnp.where(lane < 64, pltpu.roll(c0, 64, 1), c1)
            v12 = jnp.concatenate([x, y[0:4]], axis=0)
            v24 = jnp.concatenate([v12, v12], axis=0)
            vals.append(jnp.concatenate([v24, v24], axis=0))
        vhi, vlo = split2(jnp.concatenate(vals, axis=1))
        idx = lanes_of_rows(fn_s, 4 * g, 4)
        idx = jnp.where(idx >= nodes, 1 << 20, idx)
        oh = one_hot(jnp.bitwise_and(idx, 255), width)
        high = jnp.minimum(lax.shift_right_logical(idx, 8), 200)
        hb = (jnp.broadcast_to(high, (48, width)) - sub12).astype(F32).astype(BF16)
        zero = jnp.zeros((48, width), BF16)
        lhs = []
        for q in range(10):
            mask = hb == jnp.asarray(4 * q, BF16)
            lhs.append(halves(jnp.where(mask, vhi, zero), jnp.where(mask, vlo, zero)))
        res = lax.dot_general(
            jnp.concatenate(lhs, axis=0),
            halves(oh, oh),
            (((1,), (1,)), ((), ())),
            preferred_element_type=F32,
        )
        dep_s[0] += res[:, 0:128]
        dep_s[1] += res[:, 128:256]
        return carry

    lax.fori_loop(0, 16, deposit, 0)

    for n in range(4):
        sides = []
        for side in range(2):
            parts = [dep_s[side, pl.ds(3 * n + c, 40, stride=12), :] for c in range(3)]
            sides.append(jnp.concatenate(parts + [jnp.zeros((8, 128), F32)], axis=0))
        hi, lo = split2(halves(sides[0], sides[1]))
        tabi_s[n, :, 0:256] = hi
        tabi_s[n, :, 256:512] = lo
    sub = lax.broadcasted_iota(jnp.int32, (8, width), 0)

    def pick_inj(n, g):
        idx = lanes_of_rows(conn_s, 4 * g, 4)
        oh = one_hot(jnp.bitwise_and(idx, 255), width)
        res = jnp.dot(
            tabi_s[n], jnp.concatenate([oh, oh], axis=0), preferred_element_type=F32
        )
        hb = jnp.broadcast_to(lax.shift_right_logical(idx, 8), (8, width)) - sub
        acc = [jnp.zeros((8, width), F32)] * 3
        for q in range(5):
            mask = hb == 8 * q
            for c in range(3):
                at = 40 * c + 8 * q
                acc[c] = jnp.where(mask, res[at : at + 8], acc[c])
        for c in range(3):
            total = jnp.sum(acc[c], axis=0, keepdims=True)
            for q in range(4):
                ie_s[pl.ds(n * 384 + c * 128 + 4 * g + q, 1), :] = total[:, 128 * q : 128 * q + 128]

    def pick_injs(n, start, stop):
        def body(g, carry):
            pick_inj(n, g)
            return carry

        lax.fori_loop(start, stop, body, 0, unroll=2)

    pick_injs(0, 0, 32)

    def step(n, carry):
        for c in range(3):
            at = slice(c * 128, c * 128 + 128)
            inj = ie_s[pl.ds(pl.multiple_of(n * 384 + c * 128, 128), 128), :]
            f_s[at, :] = f_s[at, :] + w_s[...] * inj
        for d in range(2):
            sends = []
            for side in range(2):
                part = 2 * d + side
                take_face(f_s, part, send_s.at[part])
            for side in range(2):
                part = 2 * d + side
                copy = pltpu.make_async_remote_copy(
                    src_ref=send_s.at[part],
                    dst_ref=recv_s.at[n, part ^ 1],
                    send_sem=sem_send.at[n, part],
                    recv_sem=sem_recv.at[n, part ^ 1],
                    device_id=targets[part],
                    device_id_type=MESH,
                )
                copy.start()
                sends.append(copy)
            into_low = dot3(send_s[2 * d + 1], mat_s[2 * d, 0:128, :])
            into_high = dot3(send_s[2 * d], mat_s[2 * d + 1, 0:128, :])

            @pl.when(n < 3)
            def _():
                pick_injs(n + 1, 16 * d, 16 * d + 16)

            for copy in sends:
                copy.wait()
            into_low += dot3(recv_s[n, 2 * d], mat_s[2 * d, 128:256, :])
            into_high += dot3(recv_s[n, 2 * d + 1], mat_s[2 * d + 1, 128:256, :])
            add_face(f_s, 2 * d, into_low)
            add_face(f_s, 2 * d + 1, into_high)
        local_sum(2)
        total = f_s[...]
        scale = st_s[896:1024, :]
        scale = jnp.concatenate([scale, scale, scale], axis=0)
        v = st_s[384:768, :] + total * scale
        st_s[384:768, :] = v
        st_s[0:384, :] = st_s[0:384, :] + DT * v
        w3 = jnp.concatenate([w_s[...], w_s[...], w_s[...]], axis=0)
        own = w3 * (total - ie_s[pl.ds(pl.multiple_of(n * 384, 128), 384), :])
        acc_s[0:384, :] = acc_s[0:384, :] + own
        acc_s[384:768, :] = acc_s[384:768, :] + (4 - n).astype(F32) * own

        @pl.when(n < 3)
        def _():
            element_force()

        return carry

    lax.fori_loop(0, 4, step, 0)

    val_s[...] = jnp.zeros(val_s.shape, F32)
    sub8 = lax.broadcasted_iota(jnp.int32, (16, width), 0) // 8

    def collect(g, carry):
        idx = lanes_of_rows(conn_s, 4 * g, 4)
        vals = []
        for q in range(4):
            six = acc_s[pl.ds(4 * g + q, 8, stride=128), :]
            vals.append(jnp.concatenate([six, six], axis=0))
        vhi, vlo = split2(jnp.concatenate(vals, axis=1))
        oh = one_hot(jnp.bitwise_and(idx, 255), width)
        high = jnp.minimum(lax.shift_right_logical(idx, 8), 200)
        hb = (jnp.broadcast_to(high, (16, width)) - sub8).astype(F32).astype(BF16)
        zero = jnp.zeros((16, width), BF16)
        lhs = []
        for q in range(groups // 2):
            mask = hb == jnp.asarray(2 * q, BF16)
            lhs.append(halves(jnp.where(mask, vhi, zero), jnp.where(mask, vlo, zero)))
        lhs = jnp.concatenate(lhs, axis=0)
        val_s[...] += lax.dot_general(
            lhs, halves(oh, oh), (((1,), (1,)), ((), ())), preferred_element_type=F32
        )
        return carry

    lax.fori_loop(0, 32, collect, 0, unroll=2)

    for h in range(nodes // 128):
        at = slice(h * 128, h * 128 + 128)
        lanes = slice((h % 2) * 128, (h % 2) * 128 + 128)
        big = h // 2
        inv = DT / mass_ref[h : h + 1, :]
        inj = [dep_s[h % 2, 12 * big + 3 * n : 12 * big + 3 * n + 3, :] for n in range(4)]
        vsum = inj[0] + inj[1] + inj[2] + inj[3] + val_s[8 * big : 8 * big + 3, lanes]
        usum = 4.0 * inj[0] + 3.0 * inj[1] + 2.0 * inj[2] + inj[3] + val_s[8 * big + 3 : 8 * big + 6, lanes]
        v0 = veloc_ref[:, at]
        outv_ref[:, at] = v0 + inv * vsum
        outd_ref[:, at] = disp_ref[:, at] + (4.0 * DT) * v0 + (DT * inv) * usum

    many = pl.ds(0, (devices - 1) * 9)
    pltpu.make_async_copy(rows_send.at[many], rows_got.at[many], rsem_send).wait()
    many = pl.ds(0, (devices - 1) * 8)
    pltpu.make_async_copy(pts_send.at[many], pts_got.at[many], psem_send).wait()


def local(n_slab, n_sec):
    grad, gradt, cube = gll_tables()
    vmem = pl.BlockSpec(memory_space=pltpu.VMEM)

    def run(
        coefficients,
        azimuths,
        route_rows,
        face_points,
        face_nodes,
        disp_start,
        veloc_start,
        memory_start,
        connectivity,
        x_shared,
        y_shared,
        absorbing,
        damping,
        modulus,
        masses,
    ):
        devices = n_slab * n_sec
        rows = azimuths.shape[1]
        nodes = disp_start.shape[1]
        groups = -(-nodes // 256)
        dma = pltpu.SemaphoreType.DMA
        return pl.pallas_call(
            lambda *refs: mega_kernel(n_slab, n_sec, *refs),
            out_shape=(
                jax.ShapeDtypeStruct((3, nodes), F32),
                jax.ShapeDtypeStruct((3, nodes), F32),
            ),
            in_specs=[vmem] * 18,
            out_specs=(vmem, vmem),
            scratch_shapes=[
                pltpu.VMEM((256, rows), BF16),
                pltpu.VMEM((devices * 16, 128), F32),
                pltpu.VMEM((devices * 16, 128), F32),
                pltpu.VMEM((devices * 8, 128), F32),
                pltpu.VMEM((devices * 8, 128), F32),
                pltpu.VMEM((576, 512), BF16),
                pltpu.VMEM((64, 128), jnp.int32),
                pltpu.VMEM((64, 128), jnp.int32),
                pltpu.VMEM((64, 128), jnp.int32),
                pltpu.VMEM((128, 128), jnp.int32),
                pltpu.VMEM((8, 640), jnp.int32),
                pltpu.VMEM((8, groups * 256), F32),
                pltpu.VMEM((groups * 8, 512), BF16),
                pltpu.VMEM((4, 128, 512), BF16),
                pltpu.VMEM((1024, 128), F32),
                pltpu.VMEM((1536, 128), F32),
                pltpu.VMEM((384, 384), F32),
                pltpu.VMEM((2, 480, 128), F32),
                pltpu.VMEM((groups * 8, 256), F32),
                pltpu.VMEM((384, 128), F32),
                pltpu.VMEM((96, 128), F32),
                pltpu.VMEM((96, 128), F32),
                pltpu.VMEM((128, 128), F32),
                pltpu.VMEM((1024, 128), F32),
                pltpu.VMEM((6, 256, 128), BF16),
                pltpu.VMEM((8, 128), F32),
                pltpu.VMEM((4, 8, 128), F32),
                pltpu.VMEM((4, 96, 128), F32),
                pltpu.VMEM((4, 4, 96, 128), F32),
                dma((4,)),
                dma((4,)),
                dma((4, 4)),
                dma((4, 4)),
                dma,
                dma,
                dma,
                dma,
            ],
            compiler_params=pltpu.CompilerParams(
                vmem_limit_bytes=VMEM_LIMIT, collective_id=0, has_side_effects=True
            ),
            name="slab_window",
        )(
            coefficients,
            azimuths,
            jnp.transpose(route_rows, (2, 0, 1)),
            face_points[0].T,
            face_nodes[0].T,
            disp_start,
            veloc_start,
            memory_start,
            connectivity,
            x_shared,
            y_shared,
            absorbing.reshape(1, -1),
            damping.reshape(1, -1),
            modulus.reshape(1, -1),
            masses.reshape(-1, 128),
            grad,
            gradt,
            cube,
        )

    return run


def solution(mesh):
    both = ("slab", "sec")
    return jax.shard_map(
        local(mesh.shape["slab"], mesh.shape["sec"]),
        mesh=mesh,
        in_specs=(
            P(None, None, both),
            P(None, both),
            P(both, None, None),
            P(both, None, None),
            P(both, None, None),
            P(None, both),
            P(None, both),
            P(None, None, both),
            P(None, both),
            P(None, both),
            P(None, both),
            P(both),
            P(both),
            P(both),
            P(both),
        ),
        out_specs=(P(None, both), P(None, both)),
        check_vma=False,
    )
```

```python
import math

import jax
import jax.numpy as jnp
import numpy as np
from jax import lax
from jax.experimental import pallas as pl
from jax.experimental.pallas import tpu as pltpu
from jax.sharding import PartitionSpec as P

F32 = jnp.float32
BF16 = jnp.bfloat16
HIGHEST = lax.Precision.HIGHEST
MESH = pl.DeviceIdType.MESH
DT = 0.1
VMEM_LIMIT = 56 * 2**20


def gll_tables():
    points = np.array([-1.0, -math.sqrt(3.0 / 7.0), 0.0, math.sqrt(3.0 / 7.0), 1.0])
    weights = np.array([0.1, 49.0 / 90.0, 32.0 / 45.0, 49.0 / 90.0, 0.1])
    products = np.array(
        [np.prod([points[r] - points[c] for c in range(5) if c != r]) for r in range(5)]
    )
    derivative = np.zeros((5, 5))
    for r in range(5):
        for c in range(5):
            if r != c:
                derivative[r, c] = products[r] / (products[c] * (points[r] - points[c]))
        derivative[r, r] = -derivative[r].sum()
    cube = weights[:, None, None] * weights[None, :, None] * weights[None, None, :]
    eye = np.eye(5)
    grad = np.zeros((3, 128, 128))
    grad[0, :125, :125] = np.kron(derivative, np.kron(eye, eye))
    grad[1, :125, :125] = np.kron(eye, np.kron(derivative, eye))
    grad[2, :125, :125] = np.kron(eye, np.kron(eye, derivative))
    grad = grad.reshape(384, 128).astype(np.float32)
    cube128 = np.zeros((128, 128), np.float32)
    cube128[:125] = cube.reshape(125, 1)

    def terms(x):
        hi = x.astype(jnp.bfloat16)
        return hi, (x - hi.astype(np.float32)).astype(jnp.bfloat16)

    return (
        np.concatenate(terms(grad), axis=1),
        np.concatenate(terms(np.ascontiguousarray(grad.T)), axis=0),
        cube128,
    )


def split2(x):
    hi = x.astype(BF16)
    return hi, (x - hi.astype(F32)).astype(BF16)


def halves(low, high):
    return jnp.concatenate([low, high], axis=1)


def lanes_of_rows(ref, start, count):
    return jnp.concatenate([ref[pl.ds(start + q, 1), :] for q in range(count)], axis=1)


def one_hot(low, width):
    iota = lax.broadcasted_iota(jnp.int32, (256, width), 0).astype(F32).astype(BF16)
    hit = iota == jnp.broadcast_to(low.astype(F32).astype(BF16), (256, width))
    return jnp.where(hit, jnp.ones((256, width), BF16), jnp.zeros((256, width), BF16))


X0, X4, Y0, Y4, Z0, Z4 = range(6)


def face_pieces(face):
    if face == X0:
        return [(0, 25, 1, 0)]
    if face == X4:
        return [(100, 25, 1, 0)]
    if face == Y0:
        return [(25 * i, 5, 1, 5 * i) for i in range(5)]
    if face == Y4:
        return [(25 * i + 20, 5, 1, 5 * i) for i in range(5)]
    if face == Z0:
        return [(0, 25, 5, 0)]
    return [(4, 25, 5, 0)]


def rows_at(start, count, stride):
    return pl.ds(start, count, stride=stride) if stride > 1 else pl.ds(start, count)


def take_face(f_ref, face, out_ref):
    for c in range(3):
        for start, count, stride, dst in face_pieces(face):
            out_ref[pl.ds(c * 32 + dst, count), :] = f_ref[rows_at(c * 128 + start, count, stride), :]


def add_face(f_ref, face, vals):
    for c in range(3):
        for start, count, stride, dst in face_pieces(face):
            at = rows_at(c * 128 + start, count, stride)
            f_ref[at, :] = f_ref[at, :] + vals[c * 32 + dst : c * 32 + dst + count, :]


def dot2(x, mat):
    parts = jnp.concatenate(split2(x), axis=0)
    n = x.shape[0]
    res = jnp.dot(parts, mat, preferred_element_type=F32)
    return res[0:n] + res[n : 2 * n]


def dot3(x, mat):
    hi = x.astype(BF16)
    rest = x - hi.astype(F32)
    mid, low = split2(rest)
    parts = jnp.concatenate([hi.astype(F32), mid.astype(F32), low.astype(F32)], axis=0)
    n = x.shape[0]
    res = jnp.dot(parts.astype(BF16), mat, preferred_element_type=F32)
    return res[0:n] + res[n : 2 * n] + res[2 * n : 3 * n]


def column(row):
    return jnp.broadcast_to(row, (128, 128)).T


def match(col, row, good):
    return jnp.where((col == row) & good, 1.0, 0.0).astype(BF16)


def synthesize(coef_ref, az_ref, route_ref, tr_ref, send_ref):
    rows = az_ref.shape[1]
    tr_ref[...] = jnp.zeros(tr_ref.shape, BF16)
    for blk in range(rows // 128):
        sl = slice(blk * 128, blk * 128 + 128)
        phi = az_ref[:, sl]
        c1 = jnp.cos(phi)
        s1 = jnp.sin(phi)
        acc = [coef_ref[0, :, sl]] * 8
        cm, sm = c1, s1
        for m in range(1, 9):
            cc = coef_ref[m, :, sl]
            cs = coef_ref[8 + m, :, sl]
            for a in range(8):
                acc[a] = acc[a] + cc * cm[a : a + 1, :] + cs * sm[a : a + 1, :]
            cm, sm = cm * c1 - sm * s1, sm * c1 + cm * s1
        stack = jnp.concatenate([acc[a] for a in (0, 2, 4, 6, 1, 3, 5, 7)], axis=0)
        hi, lo = split2(stack)
        tr_ref[0:96, sl] = hi
        tr_ref[128:224, sl] = lo
    lane = lax.broadcasted_iota(jnp.int32, (128, rows), 1)
    lane1 = lax.broadcasted_iota(jnp.int32, (128, 128), 1)
    for quad in range(3):
        got = []
        for c in range(4 * quad, 4 * quad + 4):
            col = jnp.concatenate([column(route_ref[c])] * (rows // 128), axis=1)
            pick = jnp.where(col == lane, 1.0, 0.0).astype(BF16)
            res = lax.dot_general(
                pick, tr_ref[...], (((1,), (1,)), ((), ())), preferred_element_type=F32
            )
            got.append(res[:, :128] + res[:, 128:])
        b1 = pltpu.roll(got[1], 96, 1)
        b2 = pltpu.roll(got[2], 64, 1)
        b3 = pltpu.roll(got[3], 32, 1)
        send_ref[pl.ds(3 * quad, 128, stride=16), :] = jnp.where(lane1 < 96, got[0], b1)
        send_ref[pl.ds(3 * quad + 1, 128, stride=16), :] = jnp.where(lane1 < 64, b1, b2)
        send_ref[pl.ds(3 * quad + 2, 128, stride=16), :] = jnp.where(lane1 < 32, b2, b3)


def paired(ref):
    two = jnp.concatenate([ref[...], ref[...]], axis=0).T
    lane = lax.broadcasted_iota(jnp.int32, (64, 128), 1)
    return jnp.where(lane < 64, two[0:64], two[64:128])


def mega_kernel(
    n_slab,
    n_sec,
    coef_ref,
    az_ref,
    route_ref,
    fp_ref,
    fn_ref,
    disp_ref,
    veloc_ref,
    mem_ref,
    conn_ref,
    xs_ref,
    ys_ref,
    absorb_ref,
    damp_ref,
    mod_ref,
    mass_ref,
    grad_ref,
    gradt_ref,
    cube_ref,
    outd_ref,
    outv_ref,
    tr_s,
    rows_send,
    rows_got,
    pts_send,
    pts_got,
    tabp_s,
    h_s,
    lo_s,
    fn_s,
    conn_s,
    sh_s,
    tab0_s,
    tabm_s,
    tabi_s,
    st_s,
    ie_s,
    m_s,
    dep_s,
    val_s,
    f_s,
    fa_s,
    fb_s,
    w_s,
    acc_s,
    mat_s,
    kown_s,
    pack_s,
    spread_s,
    face_s,
    send_s,
    recv_s,
    kd_s,
    kdgot_s,
    dia_s,
    ksem_send,
    ksem_recv,
    sem_send,
    sem_recv,
    rsem_send,
    rsem_recv,
    psem_send,
    psem_recv,
):
    slab = lax.axis_index("slab")
    sec = lax.axis_index("sec")
    me = slab * n_sec + sec
    devices = n_slab * n_sec
    nodes = disp_ref.shape[1]
    groups = -(-nodes // 256)
    nxt_x = lax.rem(slab + 1, n_slab)
    prv_x = lax.rem(slab + n_slab - 1, n_slab)
    nxt_y = lax.rem(sec + 1, n_sec)
    prv_y = lax.rem(sec + n_sec - 1, n_sec)
    targets = [(prv_x, sec), (nxt_x, sec), (slab, prv_y), (slab, nxt_y)]
    corners = [(x, y) for x in (prv_x, nxt_x) for y in (prv_y, nxt_y)]

    def place(d):
        return (d // n_sec, lax.rem(d, n_sec))

    barrier = pltpu.get_barrier_semaphore()

    def greet(j, carry):
        d = lax.rem(me + j, devices)
        pl.semaphore_signal(barrier, inc=1, device_id=place(d), device_id_type=MESH)
        return carry

    lax.fori_loop(1, devices, greet, 0)

    synthesize(coef_ref, az_ref, route_ref, tr_s, rows_send)

    pl.semaphore_wait(barrier, devices - 1)

    def send_rows(j, carry):
        d = lax.rem(me + j, devices)
        pltpu.make_async_remote_copy(
            src_ref=rows_send.at[pl.ds(d * 16, 9)],
            dst_ref=rows_got.at[pl.ds(me * 16, 9)],
            send_sem=rsem_send,
            recv_sem=rsem_recv,
            device_id=place(d),
            device_id_type=MESH,
        ).start()
        return carry

    lax.fori_loop(1, devices, send_rows, 0)
    own = pl.ds(pl.multiple_of(me * 16, 16), 16)
    rows_got[own, :] = rows_send[own, :]

    conn_s[...] = jnp.full(conn_s.shape, 1 << 20, jnp.int32)
    conn_s[0:125, :] = conn_ref[...]
    sh_s[...] = jnp.full(sh_s.shape, -1, jnp.int32)
    sh_s[0:2, 0 : xs_ref.shape[1]] = xs_ref[...]
    sh_s[2:4, 0 : ys_ref.shape[1]] = ys_ref[...]

    kown_s[...] = jnp.zeros(kown_s.shape, F32)
    for r, point in ((0, 12), (1, 112), (2, 52), (3, 72)):
        centre = conn_s[point : point + 1, :]
        best = jnp.zeros((128, 128), jnp.int32)
        for b in range(5):
            col = column(sh_s[r : r + 1, b * 128 : b * 128 + 128])
            slot = lax.broadcasted_iota(jnp.int32, (128, 128), 0) + (b * 128 + 1)
            best = jnp.maximum(best, jnp.where(col == centre, slot, 0))
        kown_s[r : r + 1, :] = jnp.max(best, axis=0, keepdims=True).astype(F32)
    lane1 = lax.broadcasted_iota(jnp.int32, (128, 128), 1).astype(F32)
    row1 = lax.broadcasted_iota(jnp.int32, (128, 128), 0).astype(F32)
    insides = (slab > 0, slab < n_slab - 1, sec > 0, sec < n_sec - 1)
    for r in range(4):
        slots = kown_s[r : r + 1, :]
        col = column(slots)
        before = jnp.where((col < slots) & (col > 0.5), 1.0, 0.0)
        rank = jnp.sum(before, axis=0, keepdims=True)
        rank = jnp.where(slots > 0.5, rank, -1000.0)
        ranks = column(rank)
        for b in range(4):
            pack_s[r, b * 128 : b * 128 + 128, :] = match(ranks + 32.0 * b, lane1, lane1 >= 0.0)
            spread_s[r, :, b * 128 : b * 128 + 128] = match(row1, rank + 32.0 * b, insides[r])

    for a in range(2):
        ky = dot3(kown_s[...], pack_s[a, 0:128, :])
        kd_s[4 * a : 4 * a + 4, :] = ky[2:6]
    dcopies = []
    for d in (2, 3):
        copy = pltpu.make_async_remote_copy(
            src_ref=kd_s,
            dst_ref=kdgot_s.at[d ^ 1],
            send_sem=ksem_send.at[d],
            recv_sem=ksem_recv.at[d ^ 1],
            device_id=targets[d],
            device_id_type=MESH,
        )
        copy.start()
        dcopies.append(copy)

    tab0_s[...] = jnp.zeros(tab0_s.shape, F32)
    tab0_s[0:3, 0:nodes] = disp_ref[...]
    tab0_s[3:6, 0:nodes] = veloc_ref[...]
    for h in range(nodes // 128):
        tab0_s[6:7, h * 128 : h * 128 + 128] = mass_ref[h : h + 1, :]
    for h2 in range(groups // 2):
        two = jnp.concatenate(
            [tab0_s[:, h2 * 512 : h2 * 512 + 256], tab0_s[:, h2 * 512 + 256 : h2 * 512 + 512]], axis=0
        )
        hi, lo = split2(two)
        tabm_s[h2 * 16 : h2 * 16 + 16, 0:256] = hi
        tabm_s[h2 * 16 : h2 * 16 + 16, 256:512] = lo

    width = 512

    def pick_state(g, carry):
        idx = lanes_of_rows(conn_s, 4 * g, 4)
        oh = one_hot(jnp.bitwise_and(idx, 255), width)
        res = jnp.dot(
            tabm_s[...], jnp.concatenate([oh, oh], axis=0), preferred_element_type=F32
        )
        hb = jnp.broadcast_to(lax.shift_right_logical(idx, 8), (8, width))
        acc = jnp.zeros((8, width), F32)
        for h in range(groups):
            acc = jnp.where(hb == h, res[8 * h : 8 * h + 8], acc)
        for q in range(4):
            st_s[pl.ds(4 * g + q, 8, stride=128), :] = acc[:, 128 * q : 128 * q + 128]
        return carry

    lax.fori_loop(0, 32, pick_state, 0, unroll=2)

    for d, (low_point, high_point) in enumerate(((12, 112), (52, 72), (60, 64))):
        low = conn_s[low_point : low_point + 1, :]
        high = conn_s[high_point : high_point + 1, :]
        mat_s[2 * d] = match(column(high), low, True)
        mat_s[2 * d + 1] = match(column(low), high, True)

    absorb = absorb_ref[...].astype(F32)
    retain = jnp.exp(-DT * damp_ref[...])
    m_s[...] = jnp.zeros(m_s.shape, F32)
    for d in range(3):
        for c in range(3):
            m_s[d * 128 : d * 128 + 125, c * 128 : c * 128 + 128] = mem_ref[3 * d + c]
    row = lax.broadcasted_iota(jnp.int32, (128, 128), 0)
    mass = st_s[768:896, :]
    st_s[896:1024, :] = jnp.where(row < 125, DT / jnp.where(row < 125, mass, 1.0), 0.0)
    acc_s[...] = jnp.zeros(acc_s.shape, F32)

    def local_sum(d):
        take_face(f_s, 2 * d, fa_s)
        take_face(f_s, 2 * d + 1, fb_s)
        into_low = dot2(fb_s[...], mat_s[2 * d])
        into_high = dot2(fa_s[...], mat_s[2 * d + 1])
        add_face(f_s, 2 * d, into_low)
        add_face(f_s, 2 * d + 1, into_high)

    fa_s[...] = jnp.zeros(fa_s.shape, F32)
    fb_s[...] = jnp.zeros(fb_s.shape, F32)
    face_s[...] = jnp.zeros(face_s.shape, F32)
    f_s[...] = jnp.ones(f_s.shape, F32)
    for d in range(3):
        local_sum(d)
    w_s[...] = 1.0 / f_s[0:128, :]

    def element_force():
        u = jnp.concatenate([st_s[c * 128 : c * 128 + 128, :] for c in range(3)], axis=1)
        uhi, ulo = split2(u)
        both = halves(uhi, ulo)
        both = jnp.dot(
            grad_ref[...], jnp.concatenate([both, both], axis=0), preferred_element_type=F32
        )
        g = both[:, 0:384] + both[:, 384:768]
        wide = lambda x: jnp.concatenate([x, x, x], axis=1)
        ab, rt = wide(absorb), wide(retain)
        weight = wide(mod_ref[...] * cube_ref[...])
        weight = jnp.concatenate([weight, weight, weight], axis=0)
        mem = m_s[...]
        stress = weight * (g - ab * mem)
        m_s[...] = ab * (rt * mem + (1.0 - rt) * g)
        shi, slo = split2(stress)
        both = jnp.dot(gradt_ref[...], halves(shi, slo), preferred_element_type=F32)
        both = both[:, 0:384] + both[:, 384:768]
        div = both[0:128] + both[128:256]
        for c in range(3):
            f_s[c * 128 : c * 128 + 128, :] = -div[:, c * 128 : c * 128 + 128]

    element_force()

    p = paired(fp_ref)
    pf = p.astype(F32)
    a = ((pf + 0.5) * (1.0 / 1536.0)).astype(jnp.int32)
    n = p - a * 1536
    s = ((n.astype(F32) + 0.5) * (1.0 / 12.0)).astype(jnp.int32)
    c = n - s * 12
    h_s[...] = jnp.where(p >= 12288, 1000, c * 4 + lax.shift_right_logical(a, 1))
    lo_s[...] = jnp.bitwise_and(a, 1) * 128 + s
    fn_s[...] = paired(fn_ref)

    many = pl.ds(0, (devices - 1) * 9)
    pltpu.make_async_copy(rows_send.at[many], rows_got.at[many], rsem_recv).wait()
    blocks = [rows_got[pl.ds(j, 128, stride=16), :].T for j in range(9)]
    blocks = jnp.concatenate(blocks, axis=0)
    for c in range(12):
        base = c * 96
        hi, lo = split2(halves(blocks[base : base + 48], blocks[base + 48 : base + 96]))
        tabp_s[c * 48 : c * 48 + 48, 0:256] = hi
        tabp_s[c * 48 : c * 48 + 48, 256:512] = lo
    sub12 = lax.broadcasted_iota(jnp.int32, (48, width), 0) // 12
    lane = lax.broadcasted_iota(jnp.int32, (8, 128), 1)

    def send_points(d):
        @pl.when(d != me)
        def _():
            pltpu.make_async_remote_copy(
                src_ref=pts_send.at[pl.ds(d * 8, 8)],
                dst_ref=pts_got.at[pl.ds(me * 8, 8)],
                send_sem=psem_send,
                recv_sem=psem_recv,
                device_id=place(d),
                device_id_type=MESH,
            ).start()

    def pick_points(k, carry):
        g = lax.rem(k + me, 16)
        oh = one_hot(lanes_of_rows(lo_s, 4 * g, 4), width)
        res = jnp.dot(
            tabp_s[...], jnp.concatenate([oh, oh], axis=0), preferred_element_type=F32
        )
        hb = jnp.broadcast_to(lanes_of_rows(h_s, 4 * g, 4), (48, width)) - sub12
        acc = jnp.zeros((48, width), F32)
        for q in range(12):
            acc = jnp.where(hb == 4 * q, res[48 * q : 48 * q + 48], acc)
        acc = acc[0:24] + acc[24:48]
        acc = acc[0:12] + acc[12:24]
        x = acc[0:8]
        y = jnp.concatenate([acc[8:12], acc[8:12]], axis=0)
        for q in range(4):
            xq = x[:, 128 * q : 128 * q + 128]
            yq = y[:, 128 * q : 128 * q + 128]
            r = (4 * g + q) * 8
            pts_send[pl.ds(pl.multiple_of(r, 8), 8), :] = jnp.where(lane < 64, xq, pltpu.roll(yq, 64, 1))
            pts_send[pl.ds(pl.multiple_of(r + 512, 8), 8), :] = jnp.where(
                lane < 64, pltpu.roll(xq, 64, 1), yq
            )
        for q in range(4):
            send_points(4 * g + q)
            send_points(4 * g + q + 64)
        return carry

    lax.fori_loop(0, 16, pick_points, 0)
    for copy in dcopies:
        copy.wait()
    for a in range(2):
        for b in range(2):
            slots = column(kdgot_s[2 + b, 4 * a + 1 - b : 4 * a + 2 - b, :])
            mine = kown_s[2 + b : 3 + b, :]
            good = (mine > 0.5) & insides[a] & insides[2 + b]
            for q in range(4):
                moved = slots if q == 0 else pltpu.roll(slots, 32 * q, 0)
                dia_s[2 * a + b, :, q * 128 : q * 128 + 128] = match(moved, mine, good)
    own = pl.ds(pl.multiple_of(me * 8, 8), 8)
    pts_got[own, :] = pts_send[own, :]
    many = pl.ds(0, (devices - 1) * 8)
    pltpu.make_async_copy(pts_send.at[many], pts_got.at[many], psem_recv).wait()

    dep_s[...] = jnp.zeros(dep_s.shape, F32)

    def deposit(g, carry):
        vals = []
        for q in range(4):
            r = (4 * g + q) * 8
            c0 = pts_got[pl.ds(pl.multiple_of(r, 8), 8), :]
            c1 = pts_got[pl.ds(pl.multiple_of(r + 512, 8), 8), :]
            x = jnp.where(lane < 64, c0, pltpu.roll(c1, 64, 1))
            y = jnp.where(lane < 64, pltpu.roll(c0, 64, 1), c1)
            v12 = jnp.concatenate([x, y[0:4]], axis=0)
            v24 = jnp.concatenate([v12, v12], axis=0)
            vals.append(jnp.concatenate([v24, v24], axis=0))
        vhi, vlo = split2(jnp.concatenate(vals, axis=1))
        idx = lanes_of_rows(fn_s, 4 * g, 4)
        idx = jnp.where(idx >= nodes, 1 << 20, idx)
        oh = one_hot(jnp.bitwise_and(idx, 255), width)
        high = jnp.minimum(lax.shift_right_logical(idx, 8), 200)
        hb = (jnp.broadcast_to(high, (48, width)) - sub12).astype(F32).astype(BF16)
        zero = jnp.zeros((48, width), BF16)
        masks = [hb == jnp.asarray(4 * q, BF16) for q in range(10)]
        lhs = [jnp.where(mask, v, zero) for v in (vhi, vlo) for mask in masks]
        res = lax.dot_general(
            jnp.concatenate(lhs, axis=0), oh, (((1,), (1,)), ((), ())), preferred_element_type=F32
        )
        res = res[0:480] + res[480:960]
        dep_s[0] += res[:, 0:128]
        dep_s[1] += res[:, 128:256]
        return carry

    lax.fori_loop(0, 16, deposit, 0, unroll=2)

    for n in range(4):
        sides = []
        for side in range(2):
            parts = [dep_s[side, pl.ds(3 * n + c, 40, stride=12), :] for c in range(3)]
            sides.append(jnp.concatenate(parts + [jnp.zeros((8, 128), F32)], axis=0))
        hi, lo = split2(halves(sides[0], sides[1]))
        tabi_s[n, 0:128, :] = hi
        tabi_s[n, 128:256, :] = lo
    sub = lax.broadcasted_iota(jnp.int32, (8, width), 0)

    def pick_inj(n, g):
        idx = lanes_of_rows(conn_s, 4 * g, 4)
        oh = one_hot(jnp.bitwise_and(idx, 255), width)
        res = jnp.dot(tabi_s[n], oh, preferred_element_type=F32)
        res = res[0:120] + res[128:248]
        hb = jnp.broadcast_to(lax.shift_right_logical(idx, 8), (8, width)) - sub
        acc = [jnp.zeros((8, width), F32)] * 3
        for q in range(5):
            mask = hb == 8 * q
            for c in range(3):
                at = 40 * c + 8 * q
                acc[c] = jnp.where(mask, res[at : at + 8], acc[c])
        for c in range(3):
            total = jnp.sum(acc[c], axis=0, keepdims=True)
            for q in range(4):
                ie_s[pl.ds(n * 384 + c * 128 + 4 * g + q, 1), :] = total[:, 128 * q : 128 * q + 128]

    def pick_injs(n, start, stop):
        def body(g, carry):
            pick_inj(n, g)
            return carry

        lax.fori_loop(start, stop, body, 0, unroll=2)

    pick_injs(0, 0, 32)

    def step(n, carry):
        for c in range(3):
            at = slice(c * 128, c * 128 + 128)
            inj = ie_s[pl.ds(pl.multiple_of(n * 384 + c * 128, 128), 128), :]
            f_s[at, :] = f_s[at, :] + w_s[...] * inj
        for d in range(3):
            local_sum(d)
        sends = []
        for part in range(4):
            take_face(f_s, part, face_s.at[part])
            face = jnp.concatenate([face_s[part, 24 * b : 24 * b + 24, :] for b in range(4)], axis=1)
            send_s[part] = dot2(face, pack_s[part])
        for part in range(8):
            corner = part - 4
            copy = pltpu.make_async_remote_copy(
                src_ref=send_s.at[part if part < 4 else corner // 2],
                dst_ref=recv_s.at[n, part ^ 1 if part < 4 else 4 + (corner ^ 3)],
                send_sem=sem_send.at[n, part],
                recv_sem=sem_recv.at[n, part ^ 1 if part < 4 else 4 + (corner ^ 3)],
                device_id=targets[part] if part < 4 else corners[corner],
                device_id_type=MESH,
            )
            copy.start()
            sends.append(copy)

        @pl.when(n < 3)
        def _():
            pick_injs(n + 1, 0, 32)

        for copy in sends:
            copy.wait()
        into = []
        for part in range(8):
            mat = spread_s[part] if part < 4 else dia_s[part - 4]
            res = dot2(recv_s[n, part], mat)
            into.append(jnp.concatenate([res[:, 128 * b : 128 * b + 128] for b in range(4)], axis=0))
        for part in range(4):
            add_face(f_s, part, into[part])
        for a in range(2):
            for b in range(2):
                for c in range(3):
                    start = c * 128 + a * 100 + b * 20
                    src = c * 32 + (1 - b) * 20
                    f_s[start : start + 5, :] = f_s[start : start + 5, :] + into[4 + 2 * a + b][src : src + 5]
        total = f_s[...]
        scale = st_s[896:1024, :]
        scale = jnp.concatenate([scale, scale, scale], axis=0)
        v = st_s[384:768, :] + total * scale
        st_s[384:768, :] = v
        st_s[0:384, :] = st_s[0:384, :] + DT * v
        w3 = jnp.concatenate([w_s[...], w_s[...], w_s[...]], axis=0)
        own = w3 * (total - ie_s[pl.ds(pl.multiple_of(n * 384, 128), 384), :])
        acc_s[0:384, :] = acc_s[0:384, :] + own
        acc_s[384:768, :] = acc_s[384:768, :] + (4 - n).astype(F32) * own

        @pl.when(n < 3)
        def _():
            element_force()

        return carry

    lax.fori_loop(0, 4, step, 0)

    val_s[...] = jnp.zeros(val_s.shape, F32)
    sub8 = lax.broadcasted_iota(jnp.int32, (16, width), 0) // 8

    def collect(g, carry):
        idx = lanes_of_rows(conn_s, 4 * g, 4)
        vals = []
        for q in range(4):
            six = acc_s[pl.ds(4 * g + q, 8, stride=128), :]
            vals.append(jnp.concatenate([six, six], axis=0))
        vhi, vlo = split2(jnp.concatenate(vals, axis=1))
        oh = one_hot(jnp.bitwise_and(idx, 255), width)
        high = jnp.minimum(lax.shift_right_logical(idx, 8), 200)
        hb = (jnp.broadcast_to(high, (16, width)) - sub8).astype(F32).astype(BF16)
        zero = jnp.zeros((16, width), BF16)
        masks = [hb == jnp.asarray(2 * q, BF16) for q in range(groups // 2)]
        lhs = [jnp.where(mask, v, zero) for v in (vhi, vlo) for mask in masks]
        res = lax.dot_general(
            jnp.concatenate(lhs, axis=0), oh, (((1,), (1,)), ((), ())), preferred_element_type=F32
        )
        val_s[...] += res[0 : groups * 8] + res[groups * 8 : groups * 16]
        return carry

    lax.fori_loop(0, 32, collect, 0, unroll=2)

    for h in range(nodes // 128):
        at = slice(h * 128, h * 128 + 128)
        lanes = slice((h % 2) * 128, (h % 2) * 128 + 128)
        big = h // 2
        inv = DT / mass_ref[h : h + 1, :]
        inj = [dep_s[h % 2, 12 * big + 3 * n : 12 * big + 3 * n + 3, :] for n in range(4)]
        vsum = inj[0] + inj[1] + inj[2] + inj[3] + val_s[8 * big : 8 * big + 3, lanes]
        usum = 4.0 * inj[0] + 3.0 * inj[1] + 2.0 * inj[2] + inj[3] + val_s[8 * big + 3 : 8 * big + 6, lanes]
        v0 = veloc_ref[:, at]
        outv_ref[:, at] = v0 + inv * vsum
        outd_ref[:, at] = disp_ref[:, at] + (4.0 * DT) * v0 + (DT * inv) * usum

    many = pl.ds(0, (devices - 1) * 9)
    pltpu.make_async_copy(rows_send.at[many], rows_got.at[many], rsem_send).wait()
    many = pl.ds(0, (devices - 1) * 8)
    pltpu.make_async_copy(pts_send.at[many], pts_got.at[many], psem_send).wait()


def local(n_slab, n_sec):
    grad, gradt, cube = gll_tables()
    vmem = pl.BlockSpec(memory_space=pltpu.VMEM)

    def run(
        coefficients,
        azimuths,
        route_rows,
        face_points,
        face_nodes,
        disp_start,
        veloc_start,
        memory_start,
        connectivity,
        x_shared,
        y_shared,
        absorbing,
        damping,
        modulus,
        masses,
    ):
        devices = n_slab * n_sec
        rows = azimuths.shape[1]
        nodes = disp_start.shape[1]
        groups = -(-nodes // 256)
        dma = pltpu.SemaphoreType.DMA
        return pl.pallas_call(
            lambda *refs: mega_kernel(n_slab, n_sec, *refs),
            out_shape=(
                jax.ShapeDtypeStruct((3, nodes), F32),
                jax.ShapeDtypeStruct((3, nodes), F32),
            ),
            in_specs=[vmem] * 18,
            out_specs=(vmem, vmem),
            scratch_shapes=[
                pltpu.VMEM((256, rows), BF16),
                pltpu.VMEM((devices * 16, 128), F32),
                pltpu.VMEM((devices * 16, 128), F32),
                pltpu.VMEM((devices * 8, 128), F32),
                pltpu.VMEM((devices * 8, 128), F32),
                pltpu.VMEM((576, 512), BF16),
                pltpu.VMEM((64, 128), jnp.int32),
                pltpu.VMEM((64, 128), jnp.int32),
                pltpu.VMEM((64, 128), jnp.int32),
                pltpu.VMEM((128, 128), jnp.int32),
                pltpu.VMEM((8, 640), jnp.int32),
                pltpu.VMEM((8, groups * 256), F32),
                pltpu.VMEM((groups * 8, 512), BF16),
                pltpu.VMEM((4, 256, 256), BF16),
                pltpu.VMEM((1024, 128), F32),
                pltpu.VMEM((1536, 128), F32),
                pltpu.VMEM((384, 384), F32),
                pltpu.VMEM((2, 480, 128), F32),
                pltpu.VMEM((groups * 8, 256), F32),
                pltpu.VMEM((384, 128), F32),
                pltpu.VMEM((96, 128), F32),
                pltpu.VMEM((96, 128), F32),
                pltpu.VMEM((128, 128), F32),
                pltpu.VMEM((1024, 128), F32),
                pltpu.VMEM((6, 128, 128), BF16),
                pltpu.VMEM((8, 128), F32),
                pltpu.VMEM((4, 512, 128), BF16),
                pltpu.VMEM((4, 128, 512), BF16),
                pltpu.VMEM((4, 96, 128), F32),
                pltpu.VMEM((4, 24, 128), F32),
                pltpu.VMEM((4, 8, 24, 128), F32),
                pltpu.VMEM((8, 128), F32),
                pltpu.VMEM((4, 8, 128), F32),
                pltpu.VMEM((4, 128, 512), BF16),
                dma((4,)),
                dma((4,)),
                dma((4, 8)),
                dma((4, 8)),
                dma,
                dma,
                dma,
                dma,
            ],
            compiler_params=pltpu.CompilerParams(
                vmem_limit_bytes=VMEM_LIMIT, collective_id=0, has_side_effects=True
            ),
            name="slab_window",
        )(
            coefficients,
            azimuths,
            jnp.transpose(route_rows, (2, 0, 1)),
            face_points[0].T,
            face_nodes[0].T,
            disp_start,
            veloc_start,
            memory_start,
            connectivity,
            x_shared,
            y_shared,
            absorbing.reshape(1, -1),
            damping.reshape(1, -1),
            modulus.reshape(1, -1),
            masses.reshape(-1, 128),
            grad,
            gradt,
            cube,
        )

    return run


def solution(mesh):
    both = ("slab", "sec")
    return jax.shard_map(
        local(mesh.shape["slab"], mesh.shape["sec"]),
        mesh=mesh,
        in_specs=(
            P(None, None, both),
            P(None, both),
            P(both, None, None),
            P(both, None, None),
            P(both, None, None),
            P(None, both),
            P(None, both),
            P(None, None, both),
            P(None, both),
            P(None, both),
            P(None, both),
            P(both),
            P(both),
            P(both),
            P(both),
        ),
        out_specs=(P(None, both), P(None, both)),
        check_vma=False,
    )
```

```python
import math

import jax
import jax.numpy as jnp
import numpy as np
from jax import lax
from jax.experimental import pallas as pl
from jax.experimental.pallas import tpu as pltpu
from jax.sharding import PartitionSpec as P

F32 = jnp.float32
BF16 = jnp.bfloat16
HIGHEST = lax.Precision.HIGHEST
MESH = pl.DeviceIdType.MESH
DT = 0.1
VMEM_LIMIT = 56 * 2**20


def gll_tables():
    points = np.array([-1.0, -math.sqrt(3.0 / 7.0), 0.0, math.sqrt(3.0 / 7.0), 1.0])
    weights = np.array([0.1, 49.0 / 90.0, 32.0 / 45.0, 49.0 / 90.0, 0.1])
    products = np.array(
        [np.prod([points[r] - points[c] for c in range(5) if c != r]) for r in range(5)]
    )
    derivative = np.zeros((5, 5))
    for r in range(5):
        for c in range(5):
            if r != c:
                derivative[r, c] = products[r] / (products[c] * (points[r] - points[c]))
        derivative[r, r] = -derivative[r].sum()
    cube = weights[:, None, None] * weights[None, :, None] * weights[None, None, :]
    eye = np.eye(5)
    grad = np.zeros((3, 128, 128))
    grad[0, :125, :125] = np.kron(derivative, np.kron(eye, eye))
    grad[1, :125, :125] = np.kron(eye, np.kron(derivative, eye))
    grad[2, :125, :125] = np.kron(eye, np.kron(eye, derivative))
    grad = grad.reshape(384, 128).astype(np.float32)
    cube128 = np.zeros((128, 128), np.float32)
    cube128[:125] = cube.reshape(125, 1)

    def terms(x):
        hi = x.astype(jnp.bfloat16)
        return hi, (x - hi.astype(np.float32)).astype(jnp.bfloat16)

    return (
        np.concatenate(terms(grad), axis=1),
        np.concatenate(terms(np.ascontiguousarray(grad.T)), axis=0),
        cube128,
    )


def split2(x):
    hi = x.astype(BF16)
    return hi, (x - hi.astype(F32)).astype(BF16)


def halves(low, high):
    return jnp.concatenate([low, high], axis=1)


def lanes_of_rows(ref, start, count):
    return jnp.concatenate([ref[pl.ds(start + q, 1), :] for q in range(count)], axis=1)


def one_hot(low, width):
    iota = lax.broadcasted_iota(jnp.int32, (256, width), 0).astype(F32).astype(BF16)
    hit = iota == jnp.broadcast_to(low.astype(F32).astype(BF16), (256, width))
    return jnp.where(hit, jnp.ones((256, width), BF16), jnp.zeros((256, width), BF16))


X0, X4, Y0, Y4, Z0, Z4 = range(6)


def face_pieces(face):
    if face == X0:
        return [(0, 25, 1, 0)]
    if face == X4:
        return [(100, 25, 1, 0)]
    if face == Y0:
        return [(25 * i, 5, 1, 5 * i) for i in range(5)]
    if face == Y4:
        return [(25 * i + 20, 5, 1, 5 * i) for i in range(5)]
    if face == Z0:
        return [(0, 25, 5, 0)]
    return [(4, 25, 5, 0)]


def rows_at(start, count, stride):
    return pl.ds(start, count, stride=stride) if stride > 1 else pl.ds(start, count)


def take_face(f_ref, face, out_ref):
    for c in range(3):
        for start, count, stride, dst in face_pieces(face):
            out_ref[pl.ds(c * 32 + dst, count), :] = f_ref[rows_at(c * 128 + start, count, stride), :]


def add_face(f_ref, face, vals):
    for c in range(3):
        for start, count, stride, dst in face_pieces(face):
            at = rows_at(c * 128 + start, count, stride)
            f_ref[at, :] = f_ref[at, :] + vals[c * 32 + dst : c * 32 + dst + count, :]


def dot2(x, mat):
    parts = jnp.concatenate(split2(x), axis=0)
    n = x.shape[0]
    res = jnp.dot(parts, mat, preferred_element_type=F32)
    return res[0:n] + res[n : 2 * n]


def dot3(x, mat):
    hi = x.astype(BF16)
    rest = x - hi.astype(F32)
    mid, low = split2(rest)
    parts = jnp.concatenate([hi.astype(F32), mid.astype(F32), low.astype(F32)], axis=0)
    n = x.shape[0]
    res = jnp.dot(parts.astype(BF16), mat, preferred_element_type=F32)
    return res[0:n] + res[n : 2 * n] + res[2 * n : 3 * n]


def column(row):
    return jnp.broadcast_to(row, (128, 128)).T


def match(col, row, good):
    return jnp.where((col == row) & good, 1.0, 0.0).astype(BF16)


def synthesize(coef_ref, az_ref, route_ref, tr_ref, send_ref):
    rows = az_ref.shape[1]
    tr_ref[...] = jnp.zeros(tr_ref.shape, BF16)
    for blk in range(rows // 128):
        sl = slice(blk * 128, blk * 128 + 128)
        phi = az_ref[:, sl]
        c1 = jnp.cos(phi)
        s1 = jnp.sin(phi)
        acc = [coef_ref[0, :, sl]] * 8
        cm, sm = c1, s1
        for m in range(1, 9):
            cc = coef_ref[m, :, sl]
            cs = coef_ref[8 + m, :, sl]
            for a in range(8):
                acc[a] = acc[a] + cc * cm[a : a + 1, :] + cs * sm[a : a + 1, :]
            cm, sm = cm * c1 - sm * s1, sm * c1 + cm * s1
        stack = jnp.concatenate([acc[a] for a in (0, 2, 4, 6, 1, 3, 5, 7)], axis=0)
        hi, lo = split2(stack)
        tr_ref[0:96, sl] = hi
        tr_ref[128:224, sl] = lo
    lane = lax.broadcasted_iota(jnp.int32, (128, rows), 1)
    lane1 = lax.broadcasted_iota(jnp.int32, (128, 128), 1)
    for quad in range(3):
        picks = []
        for c in range(4 * quad, 4 * quad + 4):
            col = jnp.concatenate([column(route_ref[c])] * (rows // 128), axis=1)
            picks.append(jnp.where(col == lane, 1.0, 0.0).astype(BF16))
        res = lax.dot_general(
            jnp.concatenate(picks, axis=0),
            tr_ref[...],
            (((1,), (1,)), ((), ())),
            preferred_element_type=F32,
        )
        res = res[:, :128] + res[:, 128:]
        got = [res[128 * c : 128 * c + 128] for c in range(4)]
        b1 = pltpu.roll(got[1], 96, 1)
        b2 = pltpu.roll(got[2], 64, 1)
        b3 = pltpu.roll(got[3], 32, 1)
        send_ref[pl.ds(3 * quad, 128, stride=16), :] = jnp.where(lane1 < 96, got[0], b1)
        send_ref[pl.ds(3 * quad + 1, 128, stride=16), :] = jnp.where(lane1 < 64, b1, b2)
        send_ref[pl.ds(3 * quad + 2, 128, stride=16), :] = jnp.where(lane1 < 32, b2, b3)


def paired(ref):
    two = jnp.concatenate([ref[...], ref[...]], axis=0).T
    lane = lax.broadcasted_iota(jnp.int32, (64, 128), 1)
    return jnp.where(lane < 64, two[0:64], two[64:128])


def mega_kernel(
    n_slab,
    n_sec,
    coef_ref,
    az_ref,
    route_ref,
    fp_ref,
    fn_ref,
    disp_ref,
    veloc_ref,
    mem_ref,
    conn_ref,
    xs_ref,
    ys_ref,
    absorb_ref,
    damp_ref,
    mod_ref,
    mass_ref,
    grad_ref,
    gradt_ref,
    cube_ref,
    acc_s,
    dep_s,
    tr_s,
    rows_send,
    rows_got,
    pts_send,
    pts_got,
    tabp_s,
    h_s,
    lo_s,
    fn_s,
    conn_s,
    sh_s,
    tab0_s,
    tabm_s,
    tabi_s,
    st_s,
    ie_s,
    m_s,
    f_s,
    fa_s,
    fb_s,
    w_s,
    mat_s,
    kown_s,
    pack_s,
    spread_s,
    face_s,
    send_s,
    recv_s,
    kd_s,
    kdgot_s,
    dia_s,
    ksem_send,
    ksem_recv,
    sem_send,
    sem_recv,
    rsem_send,
    rsem_recv,
    psem_send,
    psem_recv,
):
    slab = lax.axis_index("slab")
    sec = lax.axis_index("sec")
    me = slab * n_sec + sec
    devices = n_slab * n_sec
    nodes = disp_ref.shape[1]
    groups = -(-nodes // 256)
    nxt_x = lax.rem(slab + 1, n_slab)
    prv_x = lax.rem(slab + n_slab - 1, n_slab)
    nxt_y = lax.rem(sec + 1, n_sec)
    prv_y = lax.rem(sec + n_sec - 1, n_sec)
    targets = [(prv_x, sec), (nxt_x, sec), (slab, prv_y), (slab, nxt_y)]
    corners = [(x, y) for x in (prv_x, nxt_x) for y in (prv_y, nxt_y)]

    def place(d):
        return (d // n_sec, lax.rem(d, n_sec))

    barrier = pltpu.get_barrier_semaphore()

    def greet(j, carry):
        d = lax.rem(me + j, devices)
        pl.semaphore_signal(barrier, inc=1, device_id=place(d), device_id_type=MESH)
        return carry

    lax.fori_loop(1, devices, greet, 0)

    synthesize(coef_ref, az_ref, route_ref, tr_s, rows_send)

    pl.semaphore_wait(barrier, devices - 1)

    def send_rows(j, carry):
        d = lax.rem(me + j, devices)
        pltpu.make_async_remote_copy(
            src_ref=rows_send.at[pl.ds(d * 16, 9)],
            dst_ref=rows_got.at[pl.ds(me * 16, 9)],
            send_sem=rsem_send,
            recv_sem=rsem_recv,
            device_id=place(d),
            device_id_type=MESH,
        ).start()
        return carry

    lax.fori_loop(1, devices, send_rows, 0)
    own = pl.ds(pl.multiple_of(me * 16, 16), 16)
    rows_got[own, :] = rows_send[own, :]

    conn_s[...] = jnp.full(conn_s.shape, 1 << 20, jnp.int32)
    conn_s[0:125, :] = conn_ref[...]
    sh_s[...] = jnp.full(sh_s.shape, -1, jnp.int32)
    sh_s[0:2, 0 : xs_ref.shape[1]] = xs_ref[...]
    sh_s[2:4, 0 : ys_ref.shape[1]] = ys_ref[...]

    kown_s[...] = jnp.zeros(kown_s.shape, F32)
    for r, point in ((0, 12), (1, 112), (2, 52), (3, 72)):
        centre = conn_s[point : point + 1, :]
        best = jnp.zeros((128, 128), jnp.int32)
        for b in range(5):
            col = column(sh_s[r : r + 1, b * 128 : b * 128 + 128])
            slot = lax.broadcasted_iota(jnp.int32, (128, 128), 0) + (b * 128 + 1)
            best = jnp.maximum(best, jnp.where(col == centre, slot, 0))
        kown_s[r : r + 1, :] = jnp.max(best, axis=0, keepdims=True).astype(F32)
    lane1 = lax.broadcasted_iota(jnp.int32, (128, 128), 1).astype(F32)
    row1 = lax.broadcasted_iota(jnp.int32, (128, 128), 0).astype(F32)
    insides = (slab > 0, slab < n_slab - 1, sec > 0, sec < n_sec - 1)
    for r in range(4):
        slots = kown_s[r : r + 1, :]
        col = column(slots)
        before = jnp.where((col < slots) & (col > 0.5), 1.0, 0.0)
        rank = jnp.sum(before, axis=0, keepdims=True)
        rank = jnp.where(slots > 0.5, rank, -1000.0)
        ranks = column(rank)
        for b in range(4):
            pack_s[r, b * 128 : b * 128 + 128, :] = match(ranks + 32.0 * b, lane1, lane1 >= 0.0)
            spread_s[r, :, b * 128 : b * 128 + 128] = match(row1, rank + 32.0 * b, insides[r])

    for a in range(2):
        ky = dot3(kown_s[...], pack_s[a, 0:128, :])
        kd_s[4 * a : 4 * a + 4, :] = ky[2:6]
    dcopies = []
    for d in (2, 3):
        copy = pltpu.make_async_remote_copy(
            src_ref=kd_s,
            dst_ref=kdgot_s.at[d ^ 1],
            send_sem=ksem_send.at[d],
            recv_sem=ksem_recv.at[d ^ 1],
            device_id=targets[d],
            device_id_type=MESH,
        )
        copy.start()
        dcopies.append(copy)

    tab0_s[...] = jnp.zeros(tab0_s.shape, F32)
    tab0_s[0:3, 0:nodes] = disp_ref[...]
    tab0_s[3:6, 0:nodes] = veloc_ref[...]
    for h in range(nodes // 128):
        tab0_s[6:7, h * 128 : h * 128 + 128] = mass_ref[h : h + 1, :]
    for h2 in range(groups // 2):
        two = jnp.concatenate(
            [tab0_s[:, h2 * 512 : h2 * 512 + 256], tab0_s[:, h2 * 512 + 256 : h2 * 512 + 512]], axis=0
        )
        hi, lo = split2(two)
        tabm_s[h2 * 16 : h2 * 16 + 16, 0:256] = hi
        tabm_s[h2 * 16 : h2 * 16 + 16, 256:512] = lo

    width = 512

    def pick_state(g, carry):
        idx = lanes_of_rows(conn_s, 4 * g, 4)
        oh = one_hot(jnp.bitwise_and(idx, 255), width)
        res = jnp.dot(
            tabm_s[...], jnp.concatenate([oh, oh], axis=0), preferred_element_type=F32
        )
        hb = jnp.broadcast_to(lax.shift_right_logical(idx, 8), (8, width))
        acc = jnp.zeros((8, width), F32)
        for h in range(groups):
            acc = jnp.where(hb == h, res[8 * h : 8 * h + 8], acc)
        for q in range(4):
            st_s[pl.ds(4 * g + q, 8, stride=128), :] = acc[:, 128 * q : 128 * q + 128]
        return carry

    lax.fori_loop(0, 32, pick_state, 0, unroll=4)

    for d, (low_point, high_point) in enumerate(((12, 112), (52, 72), (60, 64))):
        low = conn_s[low_point : low_point + 1, :]
        high = conn_s[high_point : high_point + 1, :]
        mat_s[2 * d] = match(column(high), low, True)
        mat_s[2 * d + 1] = match(column(low), high, True)

    absorb = absorb_ref[...].astype(F32)
    retain = jnp.exp(-DT * damp_ref[...])
    m_s[...] = jnp.zeros(m_s.shape, F32)
    for d in range(3):
        for c in range(3):
            m_s[d * 128 : d * 128 + 125, c * 128 : c * 128 + 128] = mem_ref[3 * d + c]
    row = lax.broadcasted_iota(jnp.int32, (128, 128), 0)
    mass = st_s[768:896, :]
    st_s[896:1024, :] = jnp.where(row < 125, DT / jnp.where(row < 125, mass, 1.0), 0.0)
    acc_s[...] = jnp.zeros(acc_s.shape, F32)

    def local_sum(d):
        take_face(f_s, 2 * d, fa_s)
        take_face(f_s, 2 * d + 1, fb_s)
        into_low = dot2(fb_s[...], mat_s[2 * d])
        into_high = dot2(fa_s[...], mat_s[2 * d + 1])
        add_face(f_s, 2 * d, into_low)
        add_face(f_s, 2 * d + 1, into_high)

    fa_s[...] = jnp.zeros(fa_s.shape, F32)
    fb_s[...] = jnp.zeros(fb_s.shape, F32)
    face_s[...] = jnp.zeros(face_s.shape, F32)
    f_s[...] = jnp.ones(f_s.shape, F32)
    for d in range(3):
        local_sum(d)
    w_s[...] = 1.0 / f_s[0:128, :]

    def element_force():
        u = jnp.concatenate([st_s[c * 128 : c * 128 + 128, :] for c in range(3)], axis=1)
        uhi, ulo = split2(u)
        both = halves(uhi, ulo)
        both = jnp.dot(
            grad_ref[...], jnp.concatenate([both, both], axis=0), preferred_element_type=F32
        )
        g = both[:, 0:384] + both[:, 384:768]
        wide = lambda x: jnp.concatenate([x, x, x], axis=1)
        ab, rt = wide(absorb), wide(retain)
        weight = wide(mod_ref[...] * cube_ref[...])
        weight = jnp.concatenate([weight, weight, weight], axis=0)
        mem = m_s[...]
        stress = weight * (g - ab * mem)
        m_s[...] = ab * (rt * mem + (1.0 - rt) * g)
        shi, slo = split2(stress)
        both = jnp.dot(gradt_ref[...], halves(shi, slo), preferred_element_type=F32)
        both = both[:, 0:384] + both[:, 384:768]
        div = both[0:128] + both[128:256]
        for c in range(3):
            f_s[c * 128 : c * 128 + 128, :] = -div[:, c * 128 : c * 128 + 128]

    element_force()

    p = paired(fp_ref)
    pf = p.astype(F32)
    a = ((pf + 0.5) * (1.0 / 1536.0)).astype(jnp.int32)
    n = p - a * 1536
    s = ((n.astype(F32) + 0.5) * (1.0 / 12.0)).astype(jnp.int32)
    c = n - s * 12
    h_s[...] = jnp.where(p >= 12288, 1000, c * 4 + lax.shift_right_logical(a, 1))
    lo_s[...] = jnp.bitwise_and(a, 1) * 128 + s
    fn_s[...] = paired(fn_ref)

    many = pl.ds(0, (devices - 1) * 9)
    pltpu.make_async_copy(rows_send.at[many], rows_got.at[many], rsem_recv).wait()
    blocks = [rows_got[pl.ds(j, 128, stride=16), :].T for j in range(9)]
    blocks = jnp.concatenate(blocks, axis=0)
    for c in range(12):
        base = c * 96
        hi, lo = split2(halves(blocks[base : base + 48], blocks[base + 48 : base + 96]))
        tabp_s[c * 48 : c * 48 + 48, 0:256] = hi
        tabp_s[c * 48 : c * 48 + 48, 256:512] = lo
    sub12 = lax.broadcasted_iota(jnp.int32, (48, width), 0) // 12
    lane = lax.broadcasted_iota(jnp.int32, (8, 128), 1)

    def send_points(d):
        @pl.when(d != me)
        def _():
            pltpu.make_async_remote_copy(
                src_ref=pts_send.at[pl.ds(d * 8, 6)],
                dst_ref=pts_got.at[pl.ds(me * 8, 6)],
                send_sem=psem_send,
                recv_sem=psem_recv,
                device_id=place(d),
                device_id_type=MESH,
            ).start()

    def pick_points(k, carry):
        g = lax.rem(k + me, 16)
        oh = one_hot(lanes_of_rows(lo_s, 4 * g, 4), width)
        res = jnp.dot(
            tabp_s[...], jnp.concatenate([oh, oh], axis=0), preferred_element_type=F32
        )
        hb = jnp.broadcast_to(lanes_of_rows(h_s, 4 * g, 4), (48, width)) - sub12
        acc = jnp.zeros((48, width), F32)
        for q in range(12):
            acc = jnp.where(hb == 4 * q, res[48 * q : 48 * q + 48], acc)
        acc = acc[0:24] + acc[24:48]
        acc = acc[0:12] + acc[12:24]
        x = acc[0:8]
        y = jnp.concatenate([acc[6:12], acc[0:2]], axis=0)
        for q in range(4):
            xq = x[:, 128 * q : 128 * q + 128]
            yq = y[:, 128 * q : 128 * q + 128]
            r = (4 * g + q) * 8
            pts_send[pl.ds(pl.multiple_of(r, 8), 8), :] = jnp.where(lane < 64, xq, pltpu.roll(yq, 64, 1))
            pts_send[pl.ds(pl.multiple_of(r + 512, 8), 8), :] = jnp.where(
                lane < 64, pltpu.roll(xq, 64, 1), yq
            )
        for q in range(4):
            send_points(4 * g + q)
            send_points(4 * g + q + 64)
        return carry

    lax.fori_loop(0, 16, pick_points, 0, unroll=2)
    for copy in dcopies:
        copy.wait()
    for a in range(2):
        for b in range(2):
            slots = column(kdgot_s[2 + b, 4 * a + 1 - b : 4 * a + 2 - b, :])
            mine = kown_s[2 + b : 3 + b, :]
            good = (mine > 0.5) & insides[a] & insides[2 + b]
            for q in range(4):
                moved = slots if q == 0 else pltpu.roll(slots, 32 * q, 0)
                dia_s[2 * a + b, :, q * 128 : q * 128 + 128] = match(moved, mine, good)
    own = pl.ds(pl.multiple_of(me * 8, 8), 8)
    pts_got[own, :] = pts_send[own, :]
    many = pl.ds(0, (devices - 1) * 6)
    pltpu.make_async_copy(pts_send.at[many], pts_got.at[many], psem_recv).wait()

    dep_s[...] = jnp.zeros(dep_s.shape, F32)

    def deposit(g, carry):
        vals = []
        for q in range(4):
            r = (4 * g + q) * 8
            c0 = pts_got[pl.ds(pl.multiple_of(r, 8), 8), :]
            c1 = pts_got[pl.ds(pl.multiple_of(r + 512, 8), 8), :]
            x = jnp.where(lane < 64, c0, pltpu.roll(c1, 64, 1))
            y = jnp.where(lane < 64, pltpu.roll(c0, 64, 1), c1)
            v12 = jnp.concatenate([x[0:6], y[0:6]], axis=0)
            v24 = jnp.concatenate([v12, v12], axis=0)
            vals.append(jnp.concatenate([v24, v24], axis=0))
        vhi, vlo = split2(jnp.concatenate(vals, axis=1))
        idx = lanes_of_rows(fn_s, 4 * g, 4)
        idx = jnp.where(idx >= nodes, 1 << 20, idx)
        oh = one_hot(jnp.bitwise_and(idx, 255), width)
        high = jnp.minimum(lax.shift_right_logical(idx, 8), 200)
        hb = (jnp.broadcast_to(high, (48, width)) - sub12).astype(F32).astype(BF16)
        zero = jnp.zeros((48, width), BF16)
        masks = [hb == jnp.asarray(4 * q, BF16) for q in range(10)]
        lhs = [jnp.where(mask, v, zero) for v in (vhi, vlo) for mask in masks]
        res = lax.dot_general(
            jnp.concatenate(lhs, axis=0), oh, (((1,), (1,)), ((), ())), preferred_element_type=F32
        )
        res = res[0:480] + res[480:960]
        dep_s[0] += res[:, 0:128]
        dep_s[1] += res[:, 128:256]
        return carry

    lax.fori_loop(0, 16, deposit, 0, unroll=4)

    for n in range(4):
        sides = []
        for side in range(2):
            parts = [dep_s[side, pl.ds(3 * n + c, 40, stride=12), :] for c in range(3)]
            sides.append(jnp.concatenate(parts + [jnp.zeros((8, 128), F32)], axis=0))
        hi, lo = split2(halves(sides[0], sides[1]))
        tabi_s[n, 0:128, :] = hi
        tabi_s[n, 128:256, :] = lo
    sub = lax.broadcasted_iota(jnp.int32, (8, width), 0)

    def pick_inj(n, g):
        idx = lanes_of_rows(conn_s, 4 * g, 4)
        oh = one_hot(jnp.bitwise_and(idx, 255), width)
        res = jnp.dot(tabi_s[n], oh, preferred_element_type=F32)
        res = res[0:120] + res[128:248]
        hb = jnp.broadcast_to(lax.shift_right_logical(idx, 8), (8, width)) - sub
        acc = [jnp.zeros((8, width), F32)] * 3
        for q in range(5):
            mask = hb == 8 * q
            for c in range(3):
                at = 40 * c + 8 * q
                acc[c] = jnp.where(mask, res[at : at + 8], acc[c])
        for c in range(3):
            total = jnp.sum(acc[c], axis=0, keepdims=True)
            for q in range(4):
                ie_s[pl.ds(n * 384 + c * 128 + 4 * g + q, 1), :] = total[:, 128 * q : 128 * q + 128]

    def pick_injs(n, start, stop):
        def body(g, carry):
            pick_inj(n, g)
            return carry

        lax.fori_loop(start, stop, body, 0, unroll=8)

    pick_injs(0, 0, 32)

    def exchange(n, part):
        corner = part - 4
        into = part ^ 1 if part < 4 else 4 + (corner ^ 3)
        return pltpu.make_async_remote_copy(
            src_ref=send_s.at[n, part if part < 4 else corner // 2],
            dst_ref=recv_s.at[n, into],
            send_sem=sem_send.at[n, part],
            recv_sem=sem_recv.at[n, into],
            device_id=targets[part] if part < 4 else corners[corner],
            device_id_type=MESH,
        )

    def step(n, carry):
        for c in range(3):
            at = slice(c * 128, c * 128 + 128)
            inj = ie_s[pl.ds(pl.multiple_of(n * 384 + c * 128, 128), 128), :]
            f_s[at, :] = f_s[at, :] + w_s[...] * inj
        for d in range(3):
            local_sum(d)
        for part in range(4):
            take_face(f_s, part, face_s.at[part])
            face = jnp.concatenate([face_s[part, 24 * b : 24 * b + 24, :] for b in range(4)], axis=1)
            send_s[n, part] = dot2(face, pack_s[part])
            for to in (part, 2 * part + 4, 2 * part + 5) if part < 2 else (part,):
                exchange(n, to).start()

        @pl.when(n < 3)
        def _():
            pick_injs(n + 1, 0, 32)

        into = []
        for part in range(8):
            exchange(n, part ^ 1 if part < 4 else 4 + ((part - 4) ^ 3)).wait_recv()
            mat = spread_s[part] if part < 4 else dia_s[part - 4]
            res = dot2(recv_s[n, part], mat)
            into.append(jnp.concatenate([res[:, 128 * b : 128 * b + 128] for b in range(4)], axis=0))
        for part in range(4):
            add_face(f_s, part, into[part])
        for a in range(2):
            for b in range(2):
                for c in range(3):
                    start = c * 128 + a * 100 + b * 20
                    src = c * 32 + (1 - b) * 20
                    f_s[start : start + 5, :] = f_s[start : start + 5, :] + into[4 + 2 * a + b][src : src + 5]
        total = f_s[...]
        scale = st_s[896:1024, :]
        scale = jnp.concatenate([scale, scale, scale], axis=0)
        v = st_s[384:768, :] + total * scale
        st_s[384:768, :] = v
        st_s[0:384, :] = st_s[0:384, :] + DT * v
        w3 = jnp.concatenate([w_s[...], w_s[...], w_s[...]], axis=0)
        own = w3 * (total - ie_s[pl.ds(pl.multiple_of(n * 384, 128), 384), :])
        acc_s[0:384, :] = acc_s[0:384, :] + own
        acc_s[384:768, :] = acc_s[384:768, :] + (4 - n).astype(F32) * own

        @pl.when(n < 3)
        def _():
            element_force()

        return carry

    lax.fori_loop(0, 4, step, 0)
    for n in range(4):
        for part in range(8):
            exchange(n, part).wait_send()

    many = pl.ds(0, (devices - 1) * 9)
    pltpu.make_async_copy(rows_send.at[many], rows_got.at[many], rsem_send).wait()
    many = pl.ds(0, (devices - 1) * 6)
    pltpu.make_async_copy(pts_send.at[many], pts_got.at[many], psem_send).wait()


def collect_kernel(acc_s, dep_s, conn_ref, disp_ref, veloc_ref, mass_ref, outd_ref, outv_ref, conn_s, val_s):
    nodes = disp_ref.shape[1]
    groups = -(-nodes // 256)
    conn_s[...] = jnp.full(conn_s.shape, 1 << 20, jnp.int32)
    conn_s[0:125, :] = conn_ref[...]

    val_s[...] = jnp.zeros(val_s.shape, F32)
    sub8 = lax.broadcasted_iota(jnp.int32, (16, 512), 0) // 8

    def collect(g, carry):
        idx = lanes_of_rows(conn_s, 4 * g, 4)
        vals = []
        for q in range(4):
            six = acc_s[pl.ds(4 * g + q, 8, stride=128), :]
            vals.append(jnp.concatenate([six, six], axis=0))
        vhi, vlo = split2(jnp.concatenate(vals, axis=1))
        oh = one_hot(jnp.bitwise_and(idx, 255), 512)
        high = jnp.minimum(lax.shift_right_logical(idx, 8), 200)
        hb = (jnp.broadcast_to(high, (16, 512)) - sub8).astype(F32).astype(BF16)
        zero = jnp.zeros((16, 512), BF16)
        masks = [hb == jnp.asarray(2 * q, BF16) for q in range(groups // 2)]
        lhs = [jnp.where(mask, v, zero) for v in (vhi, vlo) for mask in masks]
        res = lax.dot_general(
            jnp.concatenate(lhs, axis=0), oh, (((1,), (1,)), ((), ())), preferred_element_type=F32
        )
        val_s[...] += res[0 : groups * 8] + res[groups * 8 : groups * 16]
        return carry

    lax.fori_loop(0, 32, collect, 0, unroll=8)

    for h in range(nodes // 128):
        at = slice(h * 128, h * 128 + 128)
        lanes = slice((h % 2) * 128, (h % 2) * 128 + 128)
        big = h // 2
        inv = DT / mass_ref[h : h + 1, :]
        inj = [dep_s[h % 2, 12 * big + 3 * n : 12 * big + 3 * n + 3, :] for n in range(4)]
        vsum = inj[0] + inj[1] + inj[2] + inj[3] + val_s[8 * big : 8 * big + 3, lanes]
        usum = 4.0 * inj[0] + 3.0 * inj[1] + 2.0 * inj[2] + inj[3] + val_s[8 * big + 3 : 8 * big + 6, lanes]
        v0 = veloc_ref[:, at]
        outv_ref[:, at] = v0 + inv * vsum
        outd_ref[:, at] = disp_ref[:, at] + (4.0 * DT) * v0 + (DT * inv) * usum


def local(n_slab, n_sec):
    grad, gradt, cube = gll_tables()
    vmem = pl.BlockSpec(memory_space=pltpu.VMEM)

    def run(
        coefficients,
        azimuths,
        route_rows,
        face_points,
        face_nodes,
        disp_start,
        veloc_start,
        memory_start,
        connectivity,
        x_shared,
        y_shared,
        absorbing,
        damping,
        modulus,
        masses,
    ):
        devices = n_slab * n_sec
        rows = azimuths.shape[1]
        nodes = disp_start.shape[1]
        groups = -(-nodes // 256)
        dma = pltpu.SemaphoreType.DMA
        mass_rows = masses.reshape(-1, 128)
        sums, injected = pl.pallas_call(
            lambda *refs: mega_kernel(n_slab, n_sec, *refs),
            out_shape=(
                jax.ShapeDtypeStruct((1024, 128), F32),
                jax.ShapeDtypeStruct((2, 480, 128), F32),
            ),
            in_specs=[vmem] * 18,
            out_specs=(vmem, vmem),
            scratch_shapes=[
                pltpu.VMEM((256, rows), BF16),
                pltpu.VMEM((devices * 16, 128), F32),
                pltpu.VMEM((devices * 16, 128), F32),
                pltpu.VMEM((devices * 8, 128), F32),
                pltpu.VMEM((devices * 8, 128), F32),
                pltpu.VMEM((576, 512), BF16),
                pltpu.VMEM((64, 128), jnp.int32),
                pltpu.VMEM((64, 128), jnp.int32),
                pltpu.VMEM((64, 128), jnp.int32),
                pltpu.VMEM((128, 128), jnp.int32),
                pltpu.VMEM((8, 640), jnp.int32),
                pltpu.VMEM((8, groups * 256), F32),
                pltpu.VMEM((groups * 8, 512), BF16),
                pltpu.VMEM((4, 256, 256), BF16),
                pltpu.VMEM((1024, 128), F32),
                pltpu.VMEM((1536, 128), F32),
                pltpu.VMEM((384, 384), F32),
                pltpu.VMEM((384, 128), F32),
                pltpu.VMEM((96, 128), F32),
                pltpu.VMEM((96, 128), F32),
                pltpu.VMEM((128, 128), F32),
                pltpu.VMEM((6, 128, 128), BF16),
                pltpu.VMEM((8, 128), F32),
                pltpu.VMEM((4, 512, 128), BF16),
                pltpu.VMEM((4, 128, 512), BF16),
                pltpu.VMEM((4, 96, 128), F32),
                pltpu.VMEM((4, 4, 24, 128), F32),
                pltpu.VMEM((4, 8, 24, 128), F32),
                pltpu.VMEM((8, 128), F32),
                pltpu.VMEM((4, 8, 128), F32),
                pltpu.VMEM((4, 128, 512), BF16),
                dma((4,)),
                dma((4,)),
                dma((4, 8)),
                dma((4, 8)),
                dma,
                dma,
                dma,
                dma,
            ],
            compiler_params=pltpu.CompilerParams(
                vmem_limit_bytes=VMEM_LIMIT, collective_id=0, has_side_effects=True
            ),
            name="slab_window",
        )(
            coefficients,
            azimuths,
            jnp.transpose(route_rows, (2, 0, 1)),
            face_points[0].T,
            face_nodes[0].T,
            disp_start,
            veloc_start,
            memory_start,
            connectivity,
            x_shared,
            y_shared,
            absorbing.reshape(1, -1),
            damping.reshape(1, -1),
            modulus.reshape(1, -1),
            mass_rows,
            grad,
            gradt,
            cube,
        )
        return pl.pallas_call(
            collect_kernel,
            out_shape=(
                jax.ShapeDtypeStruct((3, nodes), F32),
                jax.ShapeDtypeStruct((3, nodes), F32),
            ),
            in_specs=[vmem] * 6,
            out_specs=(vmem, vmem),
            scratch_shapes=[pltpu.VMEM((128, 128), jnp.int32), pltpu.VMEM((groups * 8, 256), F32)],
            compiler_params=pltpu.CompilerParams(vmem_limit_bytes=VMEM_LIMIT),
            name="node_sums",
        )(sums, injected, connectivity, disp_start, veloc_start, mass_rows)

    return run


def solution(mesh):
    both = ("slab", "sec")
    return jax.shard_map(
        local(mesh.shape["slab"], mesh.shape["sec"]),
        mesh=mesh,
        in_specs=(
            P(None, None, both),
            P(None, both),
            P(both, None, None),
            P(both, None, None),
            P(both, None, None),
            P(None, both),
            P(None, both),
            P(None, None, both),
            P(None, both),
            P(None, both),
            P(None, both),
            P(both),
            P(both),
            P(both),
            P(both),
        ),
        out_specs=(P(None, both), P(None, both)),
        check_vma=False,
    )
```

```python
import math

import jax
import jax.numpy as jnp
import numpy as np
from jax import lax
from jax.experimental import pallas as pl
from jax.experimental.pallas import tpu as pltpu
from jax.sharding import PartitionSpec as P

F32 = jnp.float32
BF16 = jnp.bfloat16
HIGHEST = lax.Precision.HIGHEST
MESH = pl.DeviceIdType.MESH
DT = 0.1
VMEM_LIMIT = 56 * 2**20


def gll_tables():
    points = np.array([-1.0, -math.sqrt(3.0 / 7.0), 0.0, math.sqrt(3.0 / 7.0), 1.0])
    weights = np.array([0.1, 49.0 / 90.0, 32.0 / 45.0, 49.0 / 90.0, 0.1])
    products = np.array(
        [np.prod([points[r] - points[c] for c in range(5) if c != r]) for r in range(5)]
    )
    derivative = np.zeros((5, 5))
    for r in range(5):
        for c in range(5):
            if r != c:
                derivative[r, c] = products[r] / (products[c] * (points[r] - points[c]))
        derivative[r, r] = -derivative[r].sum()
    cube = weights[:, None, None] * weights[None, :, None] * weights[None, None, :]
    eye = np.eye(5)
    grad = np.zeros((3, 128, 128))
    grad[0, :125, :125] = np.kron(derivative, np.kron(eye, eye))
    grad[1, :125, :125] = np.kron(eye, np.kron(derivative, eye))
    grad[2, :125, :125] = np.kron(eye, np.kron(eye, derivative))
    grad = grad.reshape(384, 128).astype(np.float32)
    cube128 = np.zeros((128, 128), np.float32)
    cube128[:125] = cube.reshape(125, 1)

    def terms(x):
        hi = x.astype(jnp.bfloat16)
        return hi, (x - hi.astype(np.float32)).astype(jnp.bfloat16)

    return (
        np.concatenate(terms(grad), axis=1),
        np.concatenate(terms(np.ascontiguousarray(grad.T)), axis=0),
        cube128,
    )


def split2(x):
    hi = x.astype(BF16)
    return hi, (x - hi.astype(F32)).astype(BF16)


def halves(low, high):
    return jnp.concatenate([low, high], axis=1)


def lanes_of_rows(ref, start, count):
    return jnp.concatenate([ref[pl.ds(start + q, 1), :] for q in range(count)], axis=1)


def one_hot(low, width):
    iota = lax.broadcasted_iota(jnp.int32, (256, width), 0).astype(F32).astype(BF16)
    hit = iota == jnp.broadcast_to(low.astype(F32).astype(BF16), (256, width))
    return jnp.where(hit, jnp.ones((256, width), BF16), jnp.zeros((256, width), BF16))


X0, X4, Y0, Y4, Z0, Z4 = range(6)


def face_pieces(face):
    if face == X0:
        return [(0, 25, 1, 0)]
    if face == X4:
        return [(100, 25, 1, 0)]
    if face == Y0:
        return [(25 * i, 5, 1, 5 * i) for i in range(5)]
    if face == Y4:
        return [(25 * i + 20, 5, 1, 5 * i) for i in range(5)]
    if face == Z0:
        return [(0, 25, 5, 0)]
    return [(4, 25, 5, 0)]


def rows_at(start, count, stride):
    return pl.ds(start, count, stride=stride) if stride > 1 else pl.ds(start, count)


def take_face(f_ref, face, out_ref):
    for c in range(3):
        for start, count, stride, dst in face_pieces(face):
            out_ref[pl.ds(c * 32 + dst, count), :] = f_ref[rows_at(c * 128 + start, count, stride), :]


def add_face(f_ref, face, vals):
    for c in range(3):
        for start, count, stride, dst in face_pieces(face):
            at = rows_at(c * 128 + start, count, stride)
            f_ref[at, :] = f_ref[at, :] + vals[c * 32 + dst : c * 32 + dst + count, :]


def dot2(x, mat):
    parts = jnp.concatenate(split2(x), axis=0)
    n = x.shape[0]
    res = jnp.dot(parts, mat, preferred_element_type=F32)
    return res[0:n] + res[n : 2 * n]


def dot3(x, mat):
    hi = x.astype(BF16)
    rest = x - hi.astype(F32)
    mid, low = split2(rest)
    parts = jnp.concatenate([hi.astype(F32), mid.astype(F32), low.astype(F32)], axis=0)
    n = x.shape[0]
    res = jnp.dot(parts.astype(BF16), mat, preferred_element_type=F32)
    return res[0:n] + res[n : 2 * n] + res[2 * n : 3 * n]


def column(row):
    return jnp.broadcast_to(row, (128, 128)).T


def match(col, row, good):
    return jnp.where((col == row) & good, 1.0, 0.0).astype(BF16)


def synthesize(coef_ref, az_ref, route_ref, tr_ref, send_ref):
    rows = az_ref.shape[1]
    tr_ref[...] = jnp.zeros(tr_ref.shape, BF16)
    for blk in range(rows // 128):
        sl = slice(blk * 128, blk * 128 + 128)
        phi = az_ref[:, sl]
        c1 = jnp.cos(phi)
        s1 = jnp.sin(phi)
        acc = [coef_ref[0, :, sl]] * 8
        cm, sm = c1, s1
        for m in range(1, 9):
            cc = coef_ref[m, :, sl]
            cs = coef_ref[8 + m, :, sl]
            for a in range(8):
                acc[a] = acc[a] + cc * cm[a : a + 1, :] + cs * sm[a : a + 1, :]
            cm, sm = cm * c1 - sm * s1, sm * c1 + cm * s1
        stack = jnp.concatenate([acc[a] for a in (0, 2, 4, 6, 1, 3, 5, 7)], axis=0)
        hi, lo = split2(stack)
        tr_ref[0:96, sl] = hi
        tr_ref[128:224, sl] = lo
    lane = lax.broadcasted_iota(jnp.int32, (128, rows), 1)
    lane1 = lax.broadcasted_iota(jnp.int32, (128, 128), 1)
    for quad in range(3):
        picks = []
        for c in range(4 * quad, 4 * quad + 4):
            col = jnp.concatenate([column(route_ref[c])] * (rows // 128), axis=1)
            picks.append(jnp.where(col == lane, 1.0, 0.0).astype(BF16))
        res = lax.dot_general(
            jnp.concatenate(picks, axis=0),
            tr_ref[...],
            (((1,), (1,)), ((), ())),
            preferred_element_type=F32,
        )
        res = res[:, :128] + res[:, 128:]
        got = [res[128 * c : 128 * c + 128] for c in range(4)]
        b1 = pltpu.roll(got[1], 96, 1)
        b2 = pltpu.roll(got[2], 64, 1)
        b3 = pltpu.roll(got[3], 32, 1)
        send_ref[pl.ds(3 * quad, 128, stride=16), :] = jnp.where(lane1 < 96, got[0], b1)
        send_ref[pl.ds(3 * quad + 1, 128, stride=16), :] = jnp.where(lane1 < 64, b1, b2)
        send_ref[pl.ds(3 * quad + 2, 128, stride=16), :] = jnp.where(lane1 < 32, b2, b3)


def paired(ref):
    two = jnp.concatenate([ref[...], ref[...]], axis=0).T
    lane = lax.broadcasted_iota(jnp.int32, (64, 128), 1)
    return jnp.where(lane < 64, two[0:64], two[64:128])


def mega_kernel(
    n_slab,
    n_sec,
    coef_ref,
    az_ref,
    route_ref,
    fp_ref,
    fn_ref,
    disp_ref,
    veloc_ref,
    mem_ref,
    conn_ref,
    xs_ref,
    ys_ref,
    absorb_ref,
    damp_ref,
    mod_ref,
    mass_ref,
    grad_ref,
    gradt_ref,
    cube_ref,
    acc_s,
    dep_s,
    tr_s,
    rows_send,
    rows_got,
    pts_send,
    pts_got,
    tabp_s,
    h_s,
    lo_s,
    fn_s,
    conn_s,
    sh_s,
    tab0_s,
    tabm_s,
    tabi_s,
    st_s,
    ie_s,
    m_s,
    f_s,
    fa_s,
    fb_s,
    w_s,
    mat_s,
    kown_s,
    pack_s,
    spread_s,
    face_s,
    send_s,
    recv_s,
    kd_s,
    kdgot_s,
    dia_s,
    ksem_send,
    ksem_recv,
    sem_send,
    sem_recv,
    rsem_send,
    rsem_recv,
    psem_send,
    psem_recv,
):
    slab = lax.axis_index("slab")
    sec = lax.axis_index("sec")
    me = slab * n_sec + sec
    devices = n_slab * n_sec
    nodes = disp_ref.shape[1]
    groups = -(-nodes // 256)
    nxt_x = lax.rem(slab + 1, n_slab)
    prv_x = lax.rem(slab + n_slab - 1, n_slab)
    nxt_y = lax.rem(sec + 1, n_sec)
    prv_y = lax.rem(sec + n_sec - 1, n_sec)
    targets = [(prv_x, sec), (nxt_x, sec), (slab, prv_y), (slab, nxt_y)]
    corners = [(x, y) for x in (prv_x, nxt_x) for y in (prv_y, nxt_y)]

    def place(d):
        return (lax.div(d, n_sec), lax.rem(d, n_sec))

    barrier = pltpu.get_barrier_semaphore()

    def greet(j, carry):
        d = lax.rem(me + j, devices)
        pl.semaphore_signal(barrier, inc=1, device_id=place(d), device_id_type=MESH)
        return carry

    lax.fori_loop(1, devices, greet, 0)

    synthesize(coef_ref, az_ref, route_ref, tr_s, rows_send)

    pl.semaphore_wait(barrier, devices - 1)

    def send_rows(j, carry):
        d = lax.rem(me + j, devices)
        pltpu.make_async_remote_copy(
            src_ref=rows_send.at[pl.ds(d * 16, 9)],
            dst_ref=rows_got.at[pl.ds(me * 16, 9)],
            send_sem=rsem_send,
            recv_sem=rsem_recv,
            device_id=place(d),
            device_id_type=MESH,
        ).start()
        return carry

    lax.fori_loop(1, devices, send_rows, 0)
    own = pl.ds(pl.multiple_of(me * 16, 16), 16)
    rows_got[own, :] = rows_send[own, :]

    conn_s[...] = jnp.full(conn_s.shape, 1 << 20, jnp.int32)
    conn_s[0:125, :] = conn_ref[...]
    sh_s[...] = jnp.full(sh_s.shape, -1, jnp.int32)
    sh_s[0:2, 0 : xs_ref.shape[1]] = xs_ref[...]
    sh_s[2:4, 0 : ys_ref.shape[1]] = ys_ref[...]

    kown_s[...] = jnp.zeros(kown_s.shape, F32)
    for r, point in ((0, 12), (1, 112), (2, 52), (3, 72)):
        centre = conn_s[point : point + 1, :]
        best = jnp.zeros((128, 128), jnp.int32)
        for b in range(5):
            col = column(sh_s[r : r + 1, b * 128 : b * 128 + 128])
            slot = lax.broadcasted_iota(jnp.int32, (128, 128), 0) + (b * 128 + 1)
            best = jnp.maximum(best, jnp.where(col == centre, slot, 0))
        kown_s[r : r + 1, :] = jnp.max(best, axis=0, keepdims=True).astype(F32)
    lane1 = lax.broadcasted_iota(jnp.int32, (128, 128), 1).astype(F32)
    row1 = lax.broadcasted_iota(jnp.int32, (128, 128), 0).astype(F32)
    insides = (slab > 0, slab < n_slab - 1, sec > 0, sec < n_sec - 1)
    for r in range(4):
        slots = kown_s[r : r + 1, :]
        col = column(slots)
        before = jnp.where((col < slots) & (col > 0.5), 1.0, 0.0)
        rank = jnp.sum(before, axis=0, keepdims=True)
        rank = jnp.where(slots > 0.5, rank, -1000.0)
        ranks = column(rank)
        for b in range(4):
            pack_s[r, b * 128 : b * 128 + 128, :] = match(ranks + 32.0 * b, lane1, lane1 >= 0.0)
            spread_s[r, :, b * 128 : b * 128 + 128] = match(row1, rank + 32.0 * b, insides[r])

    for a in range(2):
        ky = dot3(kown_s[...], pack_s[a, 0:128, :])
        kd_s[4 * a : 4 * a + 4, :] = ky[2:6]
    dcopies = []
    for d in (2, 3):
        copy = pltpu.make_async_remote_copy(
            src_ref=kd_s,
            dst_ref=kdgot_s.at[d ^ 1],
            send_sem=ksem_send.at[d],
            recv_sem=ksem_recv.at[d ^ 1],
            device_id=targets[d],
            device_id_type=MESH,
        )
        copy.start()
        dcopies.append(copy)

    tab0_s[...] = jnp.zeros(tab0_s.shape, F32)
    tab0_s[0:3, 0:nodes] = disp_ref[...]
    tab0_s[3:6, 0:nodes] = veloc_ref[...]
    for h in range(nodes // 128):
        tab0_s[6:7, h * 128 : h * 128 + 128] = mass_ref[h : h + 1, :]
    for h2 in range(groups // 2):
        two = jnp.concatenate(
            [tab0_s[:, h2 * 512 : h2 * 512 + 256], tab0_s[:, h2 * 512 + 256 : h2 * 512 + 512]], axis=0
        )
        hi, lo = split2(two)
        tabm_s[h2 * 16 : h2 * 16 + 16, 0:256] = hi
        tabm_s[h2 * 16 : h2 * 16 + 16, 256:512] = lo

    width = 512

    def pick_state(g, carry):
        idx = lanes_of_rows(conn_s, 4 * g, 4)
        oh = one_hot(jnp.bitwise_and(idx, 255), width)
        res = jnp.dot(
            tabm_s[...], jnp.concatenate([oh, oh], axis=0), preferred_element_type=F32
        )
        hb = jnp.broadcast_to(lax.shift_right_logical(idx, 8), (8, width))
        acc = jnp.zeros((8, width), F32)
        for h in range(groups):
            acc = jnp.where(hb == h, res[8 * h : 8 * h + 8], acc)
        for q in range(4):
            st_s[pl.ds(4 * g + q, 8, stride=128), :] = acc[:, 128 * q : 128 * q + 128]
        return carry

    lax.fori_loop(0, 32, pick_state, 0, unroll=4)

    for d, (low_point, high_point) in enumerate(((12, 112), (52, 72), (60, 64))):
        low = conn_s[low_point : low_point + 1, :]
        high = conn_s[high_point : high_point + 1, :]
        mat_s[2 * d] = match(column(high), low, True)
        mat_s[2 * d + 1] = match(column(low), high, True)

    absorb = absorb_ref[...].astype(F32)
    retain = jnp.exp(-DT * damp_ref[...])
    m_s[...] = jnp.zeros(m_s.shape, F32)
    for d in range(3):
        for c in range(3):
            m_s[d * 128 : d * 128 + 125, c * 128 : c * 128 + 128] = mem_ref[3 * d + c]
    row = lax.broadcasted_iota(jnp.int32, (128, 128), 0)
    mass = st_s[768:896, :]
    st_s[896:1024, :] = jnp.where(row < 125, DT / jnp.where(row < 125, mass, 1.0), 0.0)
    acc_s[...] = jnp.zeros(acc_s.shape, F32)

    def local_sum(d):
        take_face(f_s, 2 * d, fa_s)
        take_face(f_s, 2 * d + 1, fb_s)
        into_low = dot2(fb_s[...], mat_s[2 * d])
        into_high = dot2(fa_s[...], mat_s[2 * d + 1])
        add_face(f_s, 2 * d, into_low)
        add_face(f_s, 2 * d + 1, into_high)

    fa_s[...] = jnp.zeros(fa_s.shape, F32)
    fb_s[...] = jnp.zeros(fb_s.shape, F32)
    face_s[...] = jnp.zeros(face_s.shape, F32)
    f_s[...] = jnp.ones(f_s.shape, F32)
    for d in range(3):
        local_sum(d)
    w_s[...] = 1.0 / f_s[0:128, :]

    def element_force():
        u = jnp.concatenate([st_s[c * 128 : c * 128 + 128, :] for c in range(3)], axis=1)
        uhi, ulo = split2(u)
        both = halves(uhi, ulo)
        both = jnp.dot(
            grad_ref[...], jnp.concatenate([both, both], axis=0), preferred_element_type=F32
        )
        g = both[:, 0:384] + both[:, 384:768]
        wide = lambda x: jnp.concatenate([x, x, x], axis=1)
        ab, rt = wide(absorb), wide(retain)
        weight = wide(mod_ref[...] * cube_ref[...])
        weight = jnp.concatenate([weight, weight, weight], axis=0)
        mem = m_s[...]
        stress = weight * (g - ab * mem)
        m_s[...] = ab * (rt * mem + (1.0 - rt) * g)
        shi, slo = split2(stress)
        both = jnp.dot(gradt_ref[...], halves(shi, slo), preferred_element_type=F32)
        both = both[:, 0:384] + both[:, 384:768]
        div = both[0:128] + both[128:256]
        for c in range(3):
            f_s[c * 128 : c * 128 + 128, :] = -div[:, c * 128 : c * 128 + 128]

    element_force()

    p = paired(fp_ref)
    pf = p.astype(F32)
    a = ((pf + 0.5) * (1.0 / 1536.0)).astype(jnp.int32)
    n = p - a * 1536
    s = ((n.astype(F32) + 0.5) * (1.0 / 12.0)).astype(jnp.int32)
    c = n - s * 12
    h_s[...] = jnp.where(p >= 12288, 1000, c * 4 + lax.shift_right_logical(a, 1))
    lo_s[...] = jnp.bitwise_and(a, 1) * 128 + s
    fn_s[...] = paired(fn_ref)

    many = pl.ds(0, (devices - 1) * 9)
    pltpu.make_async_copy(rows_send.at[many], rows_got.at[many], rsem_recv).wait()
    blocks = [rows_got[pl.ds(j, 128, stride=16), :].T for j in range(9)]
    blocks = jnp.concatenate(blocks, axis=0)
    for c in range(12):
        base = c * 96
        hi, lo = split2(halves(blocks[base : base + 48], blocks[base + 48 : base + 96]))
        tabp_s[c * 48 : c * 48 + 48, 0:256] = hi
        tabp_s[c * 48 : c * 48 + 48, 256:512] = lo
    sub12 = lax.broadcasted_iota(jnp.int32, (48, width), 0) // 12
    lane = lax.broadcasted_iota(jnp.int32, (8, 128), 1)

    def send_points(d):
        @pl.when(d != me)
        def _():
            pltpu.make_async_remote_copy(
                src_ref=pts_send.at[pl.ds(d * 8, 6)],
                dst_ref=pts_got.at[pl.ds(me * 8, 6)],
                send_sem=psem_send,
                recv_sem=psem_recv,
                device_id=place(d),
                device_id_type=MESH,
            ).start()

    def pick_points(k, carry):
        g = lax.rem(k + me, 16)
        oh = one_hot(lanes_of_rows(lo_s, 4 * g, 4), width)
        res = jnp.dot(
            tabp_s[...], jnp.concatenate([oh, oh], axis=0), preferred_element_type=F32
        )
        hb = jnp.broadcast_to(lanes_of_rows(h_s, 4 * g, 4), (48, width)) - sub12
        acc = jnp.zeros((48, width), F32)
        for q in range(12):
            acc = jnp.where(hb == 4 * q, res[48 * q : 48 * q + 48], acc)
        acc = acc[0:24] + acc[24:48]
        acc = acc[0:12] + acc[12:24]
        x = acc[0:8]
        y = jnp.concatenate([acc[6:12], acc[0:2]], axis=0)
        for q in range(4):
            xq = x[:, 128 * q : 128 * q + 128]
            yq = y[:, 128 * q : 128 * q + 128]
            r = (4 * g + q) * 8
            pts_send[pl.ds(pl.multiple_of(r, 8), 8), :] = jnp.where(lane < 64, xq, pltpu.roll(yq, 64, 1))
            pts_send[pl.ds(pl.multiple_of(r + 512, 8), 8), :] = jnp.where(
                lane < 64, pltpu.roll(xq, 64, 1), yq
            )
        for q in range(4):
            send_points(4 * g + q)
            send_points(4 * g + q + 64)
        return carry

    lax.fori_loop(0, 16, pick_points, 0, unroll=4)
    for copy in dcopies:
        copy.wait()
    for a in range(2):
        for b in range(2):
            slots = column(kdgot_s[2 + b, 4 * a + 1 - b : 4 * a + 2 - b, :])
            mine = kown_s[2 + b : 3 + b, :]
            good = (mine > 0.5) & insides[a] & insides[2 + b]
            for q in range(4):
                moved = slots if q == 0 else pltpu.roll(slots, 32 * q, 0)
                dia_s[2 * a + b, :, q * 128 : q * 128 + 128] = match(moved, mine, good)
    own = pl.ds(pl.multiple_of(me * 8, 8), 8)
    pts_got[own, :] = pts_send[own, :]
    many = pl.ds(0, (devices - 1) * 6)
    pltpu.make_async_copy(pts_send.at[many], pts_got.at[many], psem_recv).wait()

    dep_s[...] = jnp.zeros(dep_s.shape, F32)

    def deposit(g, carry):
        vals = []
        for q in range(4):
            r = (4 * g + q) * 8
            c0 = pts_got[pl.ds(pl.multiple_of(r, 8), 8), :]
            c1 = pts_got[pl.ds(pl.multiple_of(r + 512, 8), 8), :]
            x = jnp.where(lane < 64, c0, pltpu.roll(c1, 64, 1))
            y = jnp.where(lane < 64, pltpu.roll(c0, 64, 1), c1)
            v12 = jnp.concatenate([x[0:6], y[0:6]], axis=0)
            v24 = jnp.concatenate([v12, v12], axis=0)
            vals.append(jnp.concatenate([v24, v24], axis=0))
        vhi, vlo = split2(jnp.concatenate(vals, axis=1))
        idx = lanes_of_rows(fn_s, 4 * g, 4)
        idx = jnp.where(idx >= nodes, 1 << 20, idx)
        oh = one_hot(jnp.bitwise_and(idx, 255), width)
        high = jnp.minimum(lax.shift_right_logical(idx, 8), 200)
        hb = (jnp.broadcast_to(high, (48, width)) - sub12).astype(F32).astype(BF16)
        zero = jnp.zeros((48, width), BF16)
        masks = [hb == jnp.asarray(4 * q, BF16) for q in range(10)]
        lhs = [jnp.where(mask, v, zero) for v in (vhi, vlo) for mask in masks]
        res = lax.dot_general(
            jnp.concatenate(lhs, axis=0), oh, (((1,), (1,)), ((), ())), preferred_element_type=F32
        )
        res = res[0:480] + res[480:960]
        dep_s[0] += res[:, 0:128]
        dep_s[1] += res[:, 128:256]
        return carry

    lax.fori_loop(0, 16, deposit, 0, unroll=8)

    for n in range(4):
        sides = []
        for side in range(2):
            parts = [dep_s[side, pl.ds(3 * n + c, 40, stride=12), :] for c in range(3)]
            sides.append(jnp.concatenate(parts + [jnp.zeros((8, 128), F32)], axis=0))
        hi, lo = split2(halves(sides[0], sides[1]))
        tabi_s[n, 0:128, :] = hi
        tabi_s[n, 128:256, :] = lo
    sub = lax.broadcasted_iota(jnp.int32, (8, width), 0)

    def pick_inj(n, g):
        idx = lanes_of_rows(conn_s, 4 * g, 4)
        oh = one_hot(jnp.bitwise_and(idx, 255), width)
        res = jnp.dot(tabi_s[n], oh, preferred_element_type=F32)
        res = res[0:120] + res[128:248]
        hb = jnp.broadcast_to(lax.shift_right_logical(idx, 8), (8, width)) - sub
        acc = [jnp.zeros((8, width), F32)] * 3
        for q in range(5):
            mask = hb == 8 * q
            for c in range(3):
                at = 40 * c + 8 * q
                acc[c] = jnp.where(mask, res[at : at + 8], acc[c])
        for c in range(3):
            total = jnp.sum(acc[c], axis=0, keepdims=True)
            for q in range(4):
                ie_s[pl.ds(n * 384 + c * 128 + 4 * g + q, 1), :] = total[:, 128 * q : 128 * q + 128]

    def pick_injs(n, start, stop):
        def body(g, carry):
            pick_inj(n, g)
            return carry

        lax.fori_loop(start, stop, body, 0, unroll=8)

    pick_injs(0, 0, 32)

    def exchange(n, part):
        corner = part - 4
        into = part ^ 1 if part < 4 else 4 + (corner ^ 3)
        return pltpu.make_async_remote_copy(
            src_ref=send_s.at[n, part if part < 4 else corner // 2],
            dst_ref=recv_s.at[n, into],
            send_sem=sem_send.at[n, part],
            recv_sem=sem_recv.at[n, into],
            device_id=targets[part] if part < 4 else corners[corner],
            device_id_type=MESH,
        )

    def step(n, carry):
        for c in range(3):
            at = slice(c * 128, c * 128 + 128)
            inj = ie_s[pl.ds(pl.multiple_of(n * 384 + c * 128, 128), 128), :]
            f_s[at, :] = f_s[at, :] + w_s[...] * inj
        for d in range(3):
            local_sum(d)
        for part in range(4):
            take_face(f_s, part, face_s.at[part])
            face = jnp.concatenate([face_s[part, 24 * b : 24 * b + 24, :] for b in range(4)], axis=1)
            send_s[n, part] = dot2(face, pack_s[part])
            for to in (part, 2 * part + 4, 2 * part + 5) if part < 2 else (part,):
                exchange(n, to).start()

        @pl.when(n < 3)
        def _():
            pick_injs(n + 1, 0, 32)

        into = []
        for part in range(8):
            exchange(n, part ^ 1 if part < 4 else 4 + ((part - 4) ^ 3)).wait_recv()
            mat = spread_s[part] if part < 4 else dia_s[part - 4]
            res = dot2(recv_s[n, part], mat)
            into.append(jnp.concatenate([res[:, 128 * b : 128 * b + 128] for b in range(4)], axis=0))
        for part in range(4):
            add_face(f_s, part, into[part])
        for a in range(2):
            for b in range(2):
                for c in range(3):
                    start = c * 128 + a * 100 + b * 20
                    src = c * 32 + (1 - b) * 20
                    f_s[start : start + 5, :] = f_s[start : start + 5, :] + into[4 + 2 * a + b][src : src + 5]
        total = f_s[...]
        scale = st_s[896:1024, :]
        scale = jnp.concatenate([scale, scale, scale], axis=0)
        v = st_s[384:768, :] + total * scale
        st_s[384:768, :] = v
        st_s[0:384, :] = st_s[0:384, :] + DT * v
        w3 = jnp.concatenate([w_s[...], w_s[...], w_s[...]], axis=0)
        own = w3 * (total - ie_s[pl.ds(pl.multiple_of(n * 384, 128), 384), :])
        acc_s[0:384, :] = acc_s[0:384, :] + own
        acc_s[384:768, :] = acc_s[384:768, :] + (4 - n).astype(F32) * own

        @pl.when(n < 3)
        def _():
            element_force()

        return carry

    lax.fori_loop(0, 4, step, 0)
    for n in range(4):
        for part in range(8):
            exchange(n, part).wait_send()

    many = pl.ds(0, (devices - 1) * 9)
    pltpu.make_async_copy(rows_send.at[many], rows_got.at[many], rsem_send).wait()
    many = pl.ds(0, (devices - 1) * 6)
    pltpu.make_async_copy(pts_send.at[many], pts_got.at[many], psem_send).wait()


def collect_kernel(acc_s, dep_s, conn_ref, disp_ref, veloc_ref, mass_ref, outd_ref, outv_ref, conn_s, val_s):
    nodes = disp_ref.shape[1]
    groups = -(-nodes // 256)
    conn_s[...] = jnp.full(conn_s.shape, 1 << 20, jnp.int32)
    conn_s[0:125, :] = conn_ref[...]
    blocks = -(-groups // 8)

    val_s[...] = jnp.zeros(val_s.shape, F32)
    sub6 = lax.broadcasted_iota(jnp.int32, (48, 512), 0) // 6

    def collect(g, carry):
        idx = lanes_of_rows(conn_s, 4 * g, 4)
        vals = []
        for q in range(4):
            six = acc_s[pl.ds(4 * g + q, 8, stride=128), :]
            vals.append(six[0:6])
        val = jnp.concatenate(vals, axis=1)
        val = jnp.concatenate([val] * 4, axis=0)
        vhi, vlo = split2(jnp.concatenate([val, val], axis=0))
        oh = one_hot(jnp.bitwise_and(idx, 255), 512)
        high = jnp.minimum(lax.shift_right_logical(idx, 8), 200)
        hb = (jnp.broadcast_to(high, (48, 512)) - sub6).astype(F32).astype(BF16)
        zero = jnp.zeros((48, 512), BF16)
        masks = [hb == jnp.asarray(8 * q, BF16) for q in range(blocks)]
        lhs = [jnp.where(mask, v, zero) for v in (vhi, vlo) for mask in masks]
        res = lax.dot_general(
            jnp.concatenate(lhs, axis=0), oh, (((1,), (1,)), ((), ())), preferred_element_type=F32
        )
        val_s[...] += res[0 : blocks * 48] + res[blocks * 48 : blocks * 96]
        return carry

    lax.fori_loop(0, 32, collect, 0, unroll=8)

    for h in range(nodes // 128):
        at = slice(h * 128, h * 128 + 128)
        lanes = slice((h % 2) * 128, (h % 2) * 128 + 128)
        big = h // 2
        inv = DT / mass_ref[h : h + 1, :]
        inj = [dep_s[h % 2, 12 * big + 3 * n : 12 * big + 3 * n + 3, :] for n in range(4)]
        vsum = inj[0] + inj[1] + inj[2] + inj[3] + val_s[6 * big : 6 * big + 3, lanes]
        usum = 4.0 * inj[0] + 3.0 * inj[1] + 2.0 * inj[2] + inj[3] + val_s[6 * big + 3 : 6 * big + 6, lanes]
        v0 = veloc_ref[:, at]
        outv_ref[:, at] = v0 + inv * vsum
        outd_ref[:, at] = disp_ref[:, at] + (4.0 * DT) * v0 + (DT * inv) * usum


def local(n_slab, n_sec):
    grad, gradt, cube = gll_tables()
    vmem = pl.BlockSpec(memory_space=pltpu.VMEM)

    def run(
        coefficients,
        azimuths,
        route_rows,
        face_points,
        face_nodes,
        disp_start,
        veloc_start,
        memory_start,
        connectivity,
        x_shared,
        y_shared,
        absorbing,
        damping,
        modulus,
        masses,
    ):
        devices = n_slab * n_sec
        rows = azimuths.shape[1]
        nodes = disp_start.shape[1]
        groups = -(-nodes // 256)
        dma = pltpu.SemaphoreType.DMA
        mass_rows = masses.reshape(-1, 128)
        sums, injected = pl.pallas_call(
            lambda *refs: mega_kernel(n_slab, n_sec, *refs),
            out_shape=(
                jax.ShapeDtypeStruct((1024, 128), F32),
                jax.ShapeDtypeStruct((2, 480, 128), F32),
            ),
            in_specs=[vmem] * 18,
            out_specs=(vmem, vmem),
            scratch_shapes=[
                pltpu.VMEM((256, rows), BF16),
                pltpu.VMEM((devices * 16, 128), F32),
                pltpu.VMEM((devices * 16, 128), F32),
                pltpu.VMEM((devices * 8, 128), F32),
                pltpu.VMEM((devices * 8, 128), F32),
                pltpu.VMEM((576, 512), BF16),
                pltpu.VMEM((64, 128), jnp.int32),
                pltpu.VMEM((64, 128), jnp.int32),
                pltpu.VMEM((64, 128), jnp.int32),
                pltpu.VMEM((128, 128), jnp.int32),
                pltpu.VMEM((8, 640), jnp.int32),
                pltpu.VMEM((8, groups * 256), F32),
                pltpu.VMEM((groups * 8, 512), BF16),
                pltpu.VMEM((4, 256, 256), BF16),
                pltpu.VMEM((1024, 128), F32),
                pltpu.VMEM((1536, 128), F32),
                pltpu.VMEM((384, 384), F32),
                pltpu.VMEM((384, 128), F32),
                pltpu.VMEM((96, 128), F32),
                pltpu.VMEM((96, 128), F32),
                pltpu.VMEM((128, 128), F32),
                pltpu.VMEM((6, 128, 128), BF16),
                pltpu.VMEM((8, 128), F32),
                pltpu.VMEM((4, 512, 128), BF16),
                pltpu.VMEM((4, 128, 512), BF16),
                pltpu.VMEM((4, 96, 128), F32),
                pltpu.VMEM((4, 4, 24, 128), F32),
                pltpu.VMEM((4, 8, 24, 128), F32),
                pltpu.VMEM((8, 128), F32),
                pltpu.VMEM((4, 8, 128), F32),
                pltpu.VMEM((4, 128, 512), BF16),
                dma((4,)),
                dma((4,)),
                dma((4, 8)),
                dma((4, 8)),
                dma,
                dma,
                dma,
                dma,
            ],
            compiler_params=pltpu.CompilerParams(
                vmem_limit_bytes=VMEM_LIMIT, collective_id=0, has_side_effects=True
            ),
            name="slab_window",
        )(
            coefficients,
            azimuths,
            jnp.transpose(route_rows, (2, 0, 1)),
            face_points[0].T,
            face_nodes[0].T,
            disp_start,
            veloc_start,
            memory_start,
            connectivity,
            x_shared,
            y_shared,
            absorbing.reshape(1, -1),
            damping.reshape(1, -1),
            modulus.reshape(1, -1),
            mass_rows,
            grad,
            gradt,
            cube,
        )
        return pl.pallas_call(
            collect_kernel,
            out_shape=(
                jax.ShapeDtypeStruct((3, nodes), F32),
                jax.ShapeDtypeStruct((3, nodes), F32),
            ),
            in_specs=[vmem] * 6,
            out_specs=(vmem, vmem),
            scratch_shapes=[pltpu.VMEM((128, 128), jnp.int32), pltpu.VMEM((-(-groups // 8) * 48, 256), F32)],
            compiler_params=pltpu.CompilerParams(vmem_limit_bytes=VMEM_LIMIT),
            name="node_sums",
        )(sums, injected, connectivity, disp_start, veloc_start, mass_rows)

    return run


def solution(mesh):
    both = ("slab", "sec")
    return jax.shard_map(
        local(mesh.shape["slab"], mesh.shape["sec"]),
        mesh=mesh,
        in_specs=(
            P(None, None, both),
            P(None, both),
            P(both, None, None),
            P(both, None, None),
            P(both, None, None),
            P(None, both),
            P(None, both),
            P(None, None, both),
            P(None, both),
            P(None, both),
            P(None, both),
            P(both),
            P(both),
            P(both),
            P(both),
        ),
        out_specs=(P(None, both), P(None, both)),
        check_vma=False,
    )
```
